128 devices in a mesh: db: 32 (over x, y, core), pb: 4 (over z).
Axes of the slice: x: 4, y: 4, z: 4, core: 2. Of those that a mesh axis runs over, the one named last changes fastest.
Arguments:
- query_maps: bfloat16 [128, 256, 256], P(('db', 'pb')), may hold values from -6 to 6
- database: bfloat16 [4096, 256, 256], P(('db', 'pb')), may hold values from -6 to 6
- shortlist: int32 [128, 128], P(('db', 'pb')), may hold values from 0 to 4095, as said below
- kernel_query: bfloat16 [3, 3], replicated, may hold values from -1.5 to 1.5
- kernel_db: bfloat16 [3, 3], replicated, may hold values from -1.5 to 1.5
Outputs:
- scores: float32 [128, 128], P(('db', 'pb'))
- top_scores: float32 [128, 100], P(('db', 'pb'))
The draws below stay inside these ranges and needn't reach their ends.
Inputs may be any that keep to these rules, and one draw needn't show every extreme that they name: Within one query the ids are distinct. Among the 128 shortlist entries of the query held by device q (query q), at most 2 lie in any one shard of images (ids s * 32 to (s + 1) * 32 - 1), and some shard holds exactly 2 of them for every device.
All inputs are finite; a program needn't handle non-finite values.
Results may differ from the reference program's by a relative error of at most 0.0003.
Values may be sent and summed in bfloat16 or wider, within the bound.
No kernel may reach another device: no remote copies, remote signals or barrier semaphores. Data moves between devices by JAX's collectives and lax.ppermute only.
A program may use at most 128 MiB of HBM per device.

```python
import jax
import jax.numpy as jnp
from jax import lax

C = 256
GRID = 16
CAND = 128
TOPK = 100
Q_DEV = 1
IMG_DEV = 32
NQ = 128
DB_IMG = 4096
CAP = 2


def draw_shortlist(key, part):
    shard_count = DB_IMG // IMG_DEV
    block_count = NQ // Q_DEV
    entry_count = shard_count * CAP
    take_count = Q_DEV * CAND
    hottest = jax.random.randint(jax.random.fold_in(key, 11), (), 0, shard_count)

    def one_slots(slot_key):
        return jax.random.permutation(slot_key, IMG_DEV)[:CAP]

    def one_block(block_key):
        first_key, second_key, third_key = jax.random.split(block_key, 3)
        order = jax.random.permutation(first_key, entry_count)
        shard_entry = jnp.arange(entry_count) // CAP
        priority = order + jnp.where(shard_entry == hottest, -entry_count, 0)
        chosen = jnp.argsort(priority)[:take_count]
        chosen = chosen[jax.random.permutation(second_key, take_count)]
        shard_pick = chosen // CAP
        within = chosen % CAP
        slot_table = jax.vmap(one_slots)(jax.random.split(third_key, shard_count))
        image_ids = shard_pick * IMG_DEV + slot_table[shard_pick, within]
        return image_ids.reshape(Q_DEV, CAND)
    block_keys = jax.random.split(jax.random.fold_in(key, 12), block_count)
    return jax.vmap(one_block)(block_keys).reshape(NQ, CAND).astype(jnp.int32)


def levels(key, shape, shards, smallest, high):
    factor_of = 1.0
    for position, blocks in shards:
        heights = jax.random.uniform(jax.random.fold_in(jax.random.fold_in(key, 6), position), (blocks,), jnp.float32, smallest / len(shards), high / len(shards))
        factor_of = factor_of * jnp.repeat(jnp.exp(heights), shape[position] // blocks).reshape((-1,) + (1,) * (len(shape) - 1 - position))
    return factor_of


def bell_draw(key, dims, spread, reach, cuts=(), kind=jnp.bfloat16):
    array = jax.random.normal(key, dims, jnp.float32) * spread
    if len(cuts) > 0:
        array = levels(key, dims, cuts, -0.22, 0.18) * array
    return jnp.clip(array, min=-reach, max=reach).astype(kind)


def setup_inputs(seed: int = 0) -> dict:
    streams_of = jax.random.split(jax.random.key(seed), 6)
    query_maps = bell_draw(streams_of[0], (NQ, C, GRID * GRID), 1.0, 6.0, ((0, 128),))
    database = bell_draw(streams_of[1], (DB_IMG, C, GRID * GRID), 1.0, 6.0, ((0, 128),))
    shortlist = draw_shortlist(jax.random.fold_in(streams_of[5], 71), 0)
    kernel_query = bell_draw(streams_of[3], (3, 3), 0.33, 1.5)
    kernel_db = bell_draw(streams_of[4], (3, 3), 0.33, 1.5)
    return {"query_maps": query_maps, "database": database, "shortlist": shortlist, "kernel_query": kernel_query, "kernel_db": kernel_db}


epsilon = 1e-06
score_scale = 8.0

def unit_maps(maps):
    values = maps.astype(jnp.float32)
    squares = lax.optimization_barrier(jnp.sum(values * values, axis=1, keepdims=True))
    return (values * lax.rsqrt(squares + epsilon)).astype(jnp.bfloat16)

def reference(query_maps, database, shortlist, kernel_query, kernel_db):
    query_unit = unit_maps(query_maps)
    taps_query = kernel_query.astype(jnp.float32)
    taps_db = kernel_db.astype(jnp.float32)

    def per_query(inputs):
        query_one, image_ids = inputs
        images = unit_maps(database[image_ids.astype(jnp.int32)])
        correlation = jnp.einsum('cq,ncd->nqd', query_one.astype(jnp.float32), images.astype(jnp.float32))
        rectified = jnp.maximum(correlation, 0.0).astype(jnp.bfloat16)
        rectified = lax.optimization_barrier(rectified).astype(jnp.float32)
        grid_form = rectified.reshape(CAND, GRID, GRID, GRID, GRID)
        pad_query = jnp.pad(grid_form, ((0, 0), (1, 1), (1, 1), (0, 0), (0, 0)))
        pad_db = jnp.pad(grid_form, ((0, 0), (0, 0), (0, 0), (1, 1), (1, 1)))
        filtered = jnp.zeros_like(grid_form)
        for i in range(3):
            for j in range(3):
                filtered = filtered + taps_query[i, j] * pad_query[:, i:i + GRID, j:j + GRID, :, :]
                filtered = filtered + taps_db[i, j] * pad_db[:, :, :, i:i + GRID, j:j + GRID]
        filtered = filtered.reshape(CAND, GRID * GRID, GRID * GRID)
        return score_scale * lax.optimization_barrier(jnp.mean(lax.optimization_barrier(jnp.max(filtered, axis=1)), axis=-1))
    scores = lax.map(per_query, (query_unit, shortlist))
    top_scores = lax.top_k(scores, TOPK)[0]
    return (scores, top_scores)
```

```python
import jax
import jax.numpy as jnp
from jax import lax
from jax.experimental import pallas as pl
from jax.experimental.pallas import tpu as pltpu
from jax.sharding import Mesh, PartitionSpec as P

GRID = 16
CELLS = GRID * GRID
TOPK = 100
CAND = 128
IMAGES = 32
NODES = 64
ROWS = CELLS + 16
UNROLL = 8
SPARE = 4 * NODES

epsilon = 1e-06
score_scale = 8.0
f32 = jnp.float32
bf16 = jnp.bfloat16

MAIN = ("x", "y", "c", "z")
NODE = ("x", "y", "z")


def unit_maps(maps):
    values = maps.astype(f32)
    squares = jnp.sum(values * values, axis=1, keepdims=True)
    return (values * lax.rsqrt(squares + epsilon)).astype(bf16)


def conv_matrix(kernel):
    cell_index = jnp.arange(CELLS)
    row_out = (cell_index // GRID)[:, None]
    col_out = (cell_index % GRID)[:, None]
    row_in = (cell_index // GRID)[None, :]
    col_in = (cell_index % GRID)[None, :]
    weights = kernel.astype(f32)
    matrix = jnp.zeros((CELLS, CELLS), f32)
    for i in range(3):
        for j in range(3):
            hit = (row_in == row_out + i - 1) & (col_in == col_out + j - 1)
            matrix = matrix + weights[i, j] * hit.astype(f32)
    return matrix.astype(bf16)


def pack_kernel(query_ref, ids_ref, out_ref):
    values = query_ref[0].astype(f32)
    squares = jnp.sum(values * values, axis=0, keepdims=True)
    unit = values * lax.rsqrt(squares + epsilon)
    out_ref[0, :CELLS, :] = unit.T.astype(bf16)
    ids = ids_ref[...]
    high = lax.shift_right_logical(ids, 6).astype(f32)
    low = (ids & 63).astype(f32)
    row = jnp.concatenate([high, low], axis=1)
    first = lax.broadcasted_iota(jnp.int32, (16, 2 * CAND), 0) == 0
    out_ref[0, CELLS:, :] = jnp.where(first, jnp.broadcast_to(row, first.shape), 0.0).astype(bf16)


def pack(query_maps, shortlist):
    return pl.pallas_call(
        pack_kernel,
        out_shape=jax.ShapeDtypeStruct((1, ROWS, CELLS), bf16),
    )(query_maps, shortlist)


def pair_kernel(
    shard_ref, maps_hbm, own_hbm, other_hbm, conv_q_ref, conv_d_ref, out_ref,
    query_v, image_v, ids_v, table_v, column_v, peak_v, table_s, pair_s, sems,
):
    copies = [
        pltpu.make_async_copy(maps_hbm.at[:, pl.ds(CELLS, 16), :], ids_v, sems.at[0]),
        pltpu.make_async_copy(maps_hbm.at[:, pl.ds(0, CELLS), :], query_v, sems.at[1]),
        pltpu.make_async_copy(own_hbm, image_v.at[pl.ds(0, IMAGES)], sems.at[2]),
        pltpu.make_async_copy(other_hbm, image_v.at[pl.ds(IMAGES, IMAGES)], sems.at[3]),
    ]
    for copy in copies:
        copy.start()
    copies[0].wait()
    packed = jnp.sum(ids_v[...].astype(f32), axis=1)
    ids = packed[:, :CAND].astype(jnp.int32) * 64 + packed[:, CAND:].astype(jnp.int32)
    lane = lax.broadcasted_iota(jnp.int32, (NODES, CAND), 1)
    shard = lax.shift_right_logical(ids, 5)
    slot = ids & (IMAGES - 1)
    table = jnp.full((NODES, CAND), -1, jnp.int32)
    for side in range(2):
        held = shard == shard_ref[side]
        first = jnp.min(jnp.where(held, lane, CAND), axis=1, keepdims=True)
        last = jnp.max(jnp.where(held, lane, -1), axis=1, keepdims=True)
        last = jnp.where(last > first, last, -1)
        for which, column in ((2 * side, first), (2 * side + 1, last)):
            at = lane == column
            image = jnp.max(jnp.where(at, slot, -1), axis=1, keepdims=True)
            image = jnp.where(image >= 0, image + side * IMAGES, -1)
            table = jnp.where(lane == which, image, table)
            column_v[which] = jnp.broadcast_to(column, (NODES, CAND))
    table_v[...] = table
    move = pltpu.make_async_copy(table_v, table_s, sems.at[4])
    move.start()
    move.wait()

    def fill(query, count):
        for which in range(4):
            image = table_s[query, which]
            pair_s[count] = query * 65536 + (which * NODES + query) * 64 + jnp.maximum(image, 0)
            count = count + (image >= 0).astype(jnp.int32)
        return count

    count = lax.fori_loop(0, NODES, fill, jnp.int32(0))
    for extra in range(UNROLL):
        pair_s[count + extra] = SPARE * 64
    for copy in copies[1:]:
        copy.wait()

    def group(step, carry):
        found = []
        for part in range(UNROLL):
            code = pair_s[step * UNROLL + part]
            query = lax.shift_right_logical(code, 16)
            image = code & 63
            correlation = jnp.dot(query_v[query], image_v[image], preferred_element_type=f32)
            rectified = jnp.maximum(correlation, 0.0).astype(bf16)
            found.append((lax.shift_right_logical(code, 6) & 1023, rectified))
        for row, rectified in found:
            filtered = jnp.dot(conv_q_ref[...], rectified, preferred_element_type=f32)
            filtered = filtered + jnp.dot(rectified, conv_d_ref[...], preferred_element_type=f32)
            peak_v[pl.ds(row, 1), :] = jnp.max(filtered, axis=0, keepdims=True)
        return carry

    lax.fori_loop(0, (count + UNROLL - 1) // UNROLL, group, 0)
    total = jnp.zeros((NODES, CAND), f32)
    for which in range(4):
        peaks = peak_v[pl.ds(which * NODES, NODES), :]
        score = jnp.sum(peaks, axis=1, keepdims=True) * (score_scale / CELLS)
        total = jnp.where(lane == column_v[which], score, total)
    out_ref[...] = total


def pair_scores(shards, maps, own, other, conv_q, conv_d):
    smem = pl.BlockSpec(memory_space=pltpu.SMEM)
    vmem = pl.BlockSpec(memory_space=pltpu.VMEM)
    hbm = pl.BlockSpec(memory_space=pl.ANY)
    return pl.pallas_call(
        pair_kernel,
        out_shape=jax.ShapeDtypeStruct((NODES, CAND), f32),
        in_specs=[smem, hbm, hbm, hbm, vmem, vmem],
        out_specs=vmem,
        scratch_shapes=[
            pltpu.VMEM((NODES, CELLS, CELLS), bf16),
            pltpu.VMEM((2 * IMAGES, CELLS, CELLS), bf16),
            pltpu.VMEM((NODES, 16, CELLS), bf16),
            pltpu.VMEM((NODES, CAND), jnp.int32),
            pltpu.VMEM((4, NODES, CAND), jnp.int32),
            pltpu.VMEM((4 * NODES + 8, CELLS), f32),
            pltpu.SMEM((NODES, CAND), jnp.int32),
            pltpu.SMEM((4 * NODES + UNROLL,), jnp.int32),
            pltpu.SemaphoreType.DMA((5,)),
        ],
        compiler_params=pltpu.CompilerParams(vmem_limit_bytes=48 * 2**20),
    )(shards, maps, own, other, conv_q, conv_d)


def finish_kernel(parts_ref, scores_ref, top_ref):
    row = jnp.sum(parts_ref[...], axis=0, keepdims=True)
    scores_ref[...] = row
    across = jnp.broadcast_to(row, (CAND, CAND))
    down = across.T
    at_row = lax.broadcasted_iota(jnp.int32, (CAND, CAND), 0)
    at_col = lax.broadcasted_iota(jnp.int32, (CAND, CAND), 1)
    ahead = (across > down) | ((across == down) & (at_col < at_row))
    rank = jnp.sum(ahead.astype(f32), axis=1, keepdims=True)
    placed = jnp.where(rank == at_col.astype(f32), down, 0.0)
    top_ref[...] = jnp.sum(placed, axis=0, keepdims=True)[:, :TOPK]


def finish(parts):
    return pl.pallas_call(
        finish_kernel,
        out_shape=(
            jax.ShapeDtypeStruct((1, CAND), f32),
            jax.ShapeDtypeStruct((1, TOPK), f32),
        ),
    )(parts)


def body(query_maps, database, shortlist, kernel_query, kernel_db):
    payload = pack(query_maps, shortlist)
    maps = lax.all_gather(payload, NODE, axis=0, tiled=True)
    own = unit_maps(database)
    other = lax.ppermute(own, "c", [(0, 1), (1, 0)])
    conv_q = conv_matrix(kernel_query)
    conv_d = conv_matrix(kernel_db).T
    me = lax.axis_index("c")
    base = (lax.axis_index("x") * 4 + lax.axis_index("y")) * 8 + lax.axis_index("z")
    shards = jnp.stack([base + 4 * me, base + 4 * (1 - me)]).astype(jnp.int32)
    parts = pair_scores(shards, maps, own, other, conv_q, conv_d)
    parts = lax.all_to_all(parts, NODE, split_axis=0, concat_axis=0, tiled=True)
    return finish(parts)


def solution(mesh):
    fine = Mesh(mesh.devices.reshape(4, 4, 2, 4), MAIN)
    in_specs = (P(MAIN, None, None), P(MAIN, None, None), P(MAIN, None), P(), P())
    out_specs = (P(MAIN, None), P(MAIN, None))
    return jax.shard_map(body, mesh=fine, in_specs=in_specs, out_specs=out_specs, check_vma=False)
```

```python
import jax
import jax.numpy as jnp
from jax import lax
from jax.experimental import pallas as pl
from jax.experimental.pallas import tpu as pltpu
from jax.sharding import Mesh, PartitionSpec as P

GRID = 16
CELLS = GRID * GRID
TOPK = 100
CAND = 128
IMAGES = 32
NODES = 64
CUTS = (0, 80, 176, CELLS)
UNROLL = 8
SPARE = 4 * NODES

epsilon = 1e-06
score_scale = 8.0
f32 = jnp.float32
bf16 = jnp.bfloat16

MAIN = ("x", "y", "c", "z")
NODE = ("x", "y", "z")
ORDERS = ("xyz", "yzx", "zxy")
PLACE = {"x": 0, "y": 1, "z": 2}


def exchange_pairs(axis, near):
    pairs = []
    for x in range(4):
        for y in range(4):
            for c in range(2):
                for z in range(4):
                    at = {"x": x, "y": y, "z": z}
                    to = dict(at)
                    to[axis] = at[axis] ^ (1 if (c == 0) == near else 3)
                    pairs.append(
                        (((x * 4 + y) * 2 + c) * 4 + z, ((to["x"] * 4 + to["y"]) * 2 + c) * 4 + to["z"])
                    )
    return pairs


PAIRS = {(axis, near): exchange_pairs(axis, near) for axis in "xyz" for near in (True, False)}


def unit(values):
    squares = jnp.sum(values * values, axis=0, keepdims=True)
    return values * lax.rsqrt(squares + epsilon)


def pack_kernel(query_ref, ids_ref, out0_ref, out1_ref, out2_ref):
    maps = unit(query_ref[0].astype(f32)).T.astype(bf16)
    ids = ids_ref[...]
    high = lax.shift_right_logical(ids, 6).astype(f32)
    low = (ids & 63).astype(f32)
    row = jnp.concatenate([high, low], axis=1)
    first = lax.broadcasted_iota(jnp.int32, (16, 2 * CAND), 0) == 0
    out0_ref[0, :16, :] = jnp.where(first, jnp.broadcast_to(row, first.shape), 0.0).astype(bf16)
    out0_ref[0, 16:, :] = maps[: CUTS[1]]
    out1_ref[0] = maps[CUTS[1] : CUTS[2]]
    out2_ref[0] = maps[CUTS[2] :]


def pack(query_maps, shortlist):
    rows = (CUTS[1] + 16, CUTS[2] - CUTS[1], CUTS[3] - CUTS[2])
    return pl.pallas_call(
        pack_kernel,
        out_shape=tuple(jax.ShapeDtypeStruct((1, r, CELLS), bf16) for r in rows),
    )(query_maps, shortlist)


def images_kernel(tap_q_ref, tap_d_ref, maps_ref, unit_ref, conv_q_ref, conv_d_ref):
    for image in range(maps_ref.shape[0]):
        unit_ref[image] = unit(maps_ref[image].astype(f32)).astype(bf16)

    @pl.when(pl.program_id(0) == 0)
    def _():
        near = lax.broadcasted_iota(jnp.int32, (CELLS, CELLS), 0)
        far = lax.broadcasted_iota(jnp.int32, (CELLS, CELLS), 1)
        for tap_ref, out_ref, result, source in (
            (tap_q_ref, conv_q_ref, near, far),
            (tap_d_ref, conv_d_ref, far, near),
        ):
            down = lax.shift_right_logical(source, 4) - lax.shift_right_logical(result, 4)
            right = (source & (GRID - 1)) - (result & (GRID - 1))
            matrix = jnp.zeros((CELLS, CELLS), f32)
            for i in range(3):
                for j in range(3):
                    hit = (down == i - 1) & (right == j - 1)
                    matrix = jnp.where(hit, tap_ref[i, j], matrix)
            out_ref[...] = matrix.astype(bf16)


def prepare_images(database, tap_q, tap_d):
    block = 4
    maps = pl.BlockSpec((block, CELLS, CELLS), lambda i: (i, 0, 0))
    square = pl.BlockSpec((CELLS, CELLS), lambda i: (0, 0))
    smem = pl.BlockSpec(memory_space=pltpu.SMEM)
    square_shape = jax.ShapeDtypeStruct((CELLS, CELLS), bf16)
    return pl.pallas_call(
        images_kernel,
        grid=(database.shape[0] // block,),
        in_specs=[smem, smem, maps],
        out_specs=(maps, square, square),
        out_shape=(jax.ShapeDtypeStruct(database.shape, bf16), square_shape, square_shape),
    )(tap_q, tap_d, database)


def spread(chunks):
    held = list(chunks)
    for phase in range(3):
        axes = [order[phase] for order in ORDERS]
        near = [lax.ppermute(m, MAIN, PAIRS[axis, True]) for m, axis in zip(held, axes)]
        far = [lax.ppermute(m, MAIN, PAIRS[axis, False]) for m, axis in zip(held, axes)]
        both = [lax.ppermute(m, MAIN, PAIRS[axis, False]) for m, axis in zip(near, axes)]
        parts = list(zip(held, near, far, both))
        held = [jnp.concatenate(part, axis=0) for part in parts] if phase < 2 else parts
    return held


def pair_kernel(
    place_ref, *refs,
):
    parts, refs = refs[:12], refs[12:]
    own_hbm, other_hbm, conv_q_ref, conv_d_ref, out_ref = refs[:5]
    query_v, image_v, ids_v, table_v, column_v, peak_v, total_v, table_s, pair_s, sems = refs[5:]
    id_copies, copies = [], []
    for piece, order in enumerate(ORDERS):
        size = CUTS[piece + 1] - CUTS[piece]
        skip = 16 if piece == 0 else 0
        for last in range(4):
            for middle in range(4):
                index = [0, 0, 0]
                index[PLACE[order[0]]] = slice(None)
                index[PLACE[order[1]]] = middle
                index[PLACE[order[2]]] = last
                source = parts[4 * piece + last]
                blocks = pl.ds(4 * middle, 4)
                copies.append(
                    pltpu.make_async_copy(
                        source.at[blocks, pl.ds(skip, size), :],
                        query_v.at[*index, pl.ds(CUTS[piece], size), :],
                        sems.at[1],
                    )
                )
                if piece == 0:
                    id_copies.append(
                        pltpu.make_async_copy(
                            source.at[blocks, pl.ds(0, 16), :], ids_v.at[*index], sems.at[0]
                        )
                    )
    image_copies = [
        pltpu.make_async_copy(own_hbm, image_v.at[pl.ds(0, IMAGES)], sems.at[2]),
        pltpu.make_async_copy(other_hbm, image_v.at[pl.ds(IMAGES, IMAGES)], sems.at[3]),
    ]
    for copy in id_copies + image_copies + copies:
        copy.start()
    pltpu.make_async_copy(ids_v, ids_v, sems.at[0]).wait()
    packed = jnp.sum(ids_v[...].reshape(NODES, 16, CELLS).astype(f32), axis=1)
    ids = packed[:, :CAND].astype(jnp.int32) * 64 + packed[:, CAND:].astype(jnp.int32)
    lane = lax.broadcasted_iota(jnp.int32, (NODES, CAND), 1)
    shard = lax.shift_right_logical(ids, 5)
    slot = ids & (IMAGES - 1)
    table = jnp.full((NODES, CAND), -1, jnp.int32)
    for side in range(2):
        held = shard == place_ref[side]
        first = jnp.min(jnp.where(held, lane, CAND), axis=1, keepdims=True)
        last = jnp.max(jnp.where(held, lane, -1), axis=1, keepdims=True)
        last = jnp.where(last > first, last, -1)
        for which, column in ((2 * side, first), (2 * side + 1, last)):
            at = lane == column
            image = jnp.max(jnp.where(at, slot, -1), axis=1, keepdims=True)
            image = jnp.where(image >= 0, image + side * IMAGES, -1)
            table = jnp.where(lane == which, image, table)
            column_v[which] = jnp.broadcast_to(column, (NODES, CAND))
    table_v[...] = table
    move = pltpu.make_async_copy(table_v, table_s, sems.at[4])
    move.start()
    move.wait()

    def fill(query, count):
        for which in range(4):
            image = table_s[query, which]
            pair_s[count] = query * 65536 + (which * NODES + query) * 64 + jnp.maximum(image, 0)
            count = count + (image >= 0).astype(jnp.int32)
        return count

    count = lax.fori_loop(0, NODES, fill, jnp.int32(0))
    for extra in range(UNROLL):
        pair_s[count + extra] = SPARE * 64
    for copy in image_copies:
        copy.wait()
    pltpu.make_async_copy(query_v, query_v, sems.at[1]).wait()

    def group(step, carry):
        found = []
        for part in range(UNROLL):
            code = pair_s[step * UNROLL + part]
            node = lax.shift_right_logical(code, 16)
            query = query_v[
                lax.shift_right_logical(node, 4), lax.shift_right_logical(node, 2) & 3, node & 3
            ]
            image = code & 63
            correlation = jnp.dot(query, image_v[image], preferred_element_type=f32)
            rectified = jnp.maximum(correlation, 0.0).astype(bf16)
            found.append((lax.shift_right_logical(code, 6) & 1023, rectified))
        for row, rectified in found:
            filtered = jnp.dot(conv_q_ref[...], rectified, preferred_element_type=f32)
            filtered = filtered + jnp.dot(rectified, conv_d_ref[...], preferred_element_type=f32)
            peak_v[pl.ds(row, 1), :] = jnp.max(filtered, axis=0, keepdims=True)
        return carry

    lax.fori_loop(0, (count + UNROLL - 1) // UNROLL, group, 0)
    total = jnp.zeros((NODES, CAND), f32)
    for which in range(4):
        peaks = peak_v[pl.ds(which * NODES, NODES), :]
        score = jnp.sum(peaks, axis=1, keepdims=True) * (score_scale / CELLS)
        total = jnp.where(lane == column_v[which], score, total)
    total_v[...] = total

    def settle(query, carry):
        out_ref[pl.ds(place_ref[2 + query], 1), :] = total_v[pl.ds(query, 1), :]
        return carry

    lax.fori_loop(0, NODES, settle, 0, unroll=8)


def pair_scores(place, parts, own, other, conv_q, conv_d):
    smem = pl.BlockSpec(memory_space=pltpu.SMEM)
    vmem = pl.BlockSpec(memory_space=pltpu.VMEM)
    hbm = pl.BlockSpec(memory_space=pl.ANY)
    return pl.pallas_call(
        pair_kernel,
        out_shape=jax.ShapeDtypeStruct((NODES, CAND), f32),
        in_specs=[smem] + [hbm] * 14 + [vmem, vmem],
        out_specs=vmem,
        scratch_shapes=[
            pltpu.VMEM((4, 4, 4, CELLS, CELLS), bf16),
            pltpu.VMEM((2 * IMAGES, CELLS, CELLS), bf16),
            pltpu.VMEM((4, 4, 4, 16, CELLS), bf16),
            pltpu.VMEM((NODES, CAND), jnp.int32),
            pltpu.VMEM((4, NODES, CAND), jnp.int32),
            pltpu.VMEM((4 * NODES + 8, CELLS), f32),
            pltpu.VMEM((NODES, CAND), f32),
            pltpu.SMEM((NODES, CAND), jnp.int32),
            pltpu.SMEM((4 * NODES + UNROLL,), jnp.int32),
            pltpu.SemaphoreType.DMA((5,)),
        ],
        compiler_params=pltpu.CompilerParams(vmem_limit_bytes=48 * 2**20),
    )(place, *parts, own, other, conv_q, conv_d)


def finish_kernel(parts_ref, scores_ref, top_ref):
    row = jnp.sum(parts_ref[...], axis=0, keepdims=True)
    scores_ref[...] = row
    across = jnp.broadcast_to(row, (CAND, CAND))
    down = across.T
    at_row = lax.broadcasted_iota(jnp.int32, (CAND, CAND), 0)
    at_col = lax.broadcasted_iota(jnp.int32, (CAND, CAND), 1)
    ahead = (across > down) | ((across == down) & (at_col < at_row))
    rank = jnp.sum(ahead.astype(f32), axis=1, keepdims=True)
    placed = jnp.where(rank == at_col.astype(f32), down, 0.0)
    top_ref[...] = jnp.sum(placed, axis=0, keepdims=True)[:, :TOPK]


def finish(parts):
    return pl.pallas_call(
        finish_kernel,
        out_shape=(
            jax.ShapeDtypeStruct((1, CAND), f32),
            jax.ShapeDtypeStruct((1, TOPK), f32),
        ),
    )(parts)


def body(query_maps, database, shortlist, kernel_query, kernel_db):
    chunks = pack(query_maps, shortlist)
    own, conv_q, conv_d = prepare_images(database, kernel_query.astype(f32), kernel_db.astype(f32))
    other = lax.ppermute(own, "c", [(0, 1), (1, 0)])
    parts = spread(chunks)
    me = lax.axis_index("c")
    at = [lax.axis_index(axis) for axis in NODE]
    base = (at[0] * 4 + at[1]) * 8 + at[2]
    step = jnp.arange(4, dtype=jnp.int32)
    offset = jnp.where(me == 0, step ^ lax.shift_right_logical(step, 1), (4 - step) & 3)
    offset = jnp.where((me == 1) & (step > 0), jnp.where(step == 1, 3, jnp.where(step == 2, 1, 2)), offset)
    spot = [a ^ offset for a in at]
    order = (spot[0][:, None, None] * 4 + spot[1][None, :, None]) * 4 + spot[2][None, None, :]
    place = jnp.concatenate(
        [jnp.stack([base + 4 * me, base + 4 * (1 - me)]), order.reshape(-1)]
    ).astype(jnp.int32)
    scores = pair_scores(place, [p for part in parts for p in part], own, other, conv_q, conv_d)
    scores = lax.all_to_all(scores, NODE, split_axis=0, concat_axis=0, tiled=True)
    return finish(scores)


def solution(mesh):
    fine = Mesh(mesh.devices.reshape(4, 4, 2, 4), MAIN)
    in_specs = (P(MAIN, None, None), P(MAIN, None, None), P(MAIN, None), P(), P())
    out_specs = (P(MAIN, None), P(MAIN, None))
    return jax.shard_map(body, mesh=fine, in_specs=in_specs, out_specs=out_specs, check_vma=False)
```

```python
import jax
import jax.numpy as jnp
from jax import lax
from jax.experimental import pallas as pl
from jax.experimental.pallas import tpu as pltpu
from jax.sharding import Mesh, PartitionSpec as P

GRID = 16
CELLS = GRID * GRID
TOPK = 100
CAND = 128
IMAGES = 32
NODES = 64
CUTS = (0, 80, 176, CELLS)
UNROLL = 8
SPARE = 4 * NODES

epsilon = 1e-06
score_scale = 8.0
f32 = jnp.float32
bf16 = jnp.bfloat16

MAIN = ("x", "y", "c", "z")
NODE = ("x", "y", "z")
WHOLE = (("z", True), ("x", True), ("y", False))
LATE = (("y", True), ("z", False), ("x", False))
GROUP = 8


def exchange_pairs(axis, near):
    pairs = []
    for x in range(4):
        for y in range(4):
            for c in range(2):
                for z in range(4):
                    at = {"x": x, "y": y, "z": z}
                    to = dict(at)
                    to[axis] = at[axis] ^ (1 if (c == 0) == near else 3)
                    pairs.append(
                        (((x * 4 + y) * 2 + c) * 4 + z, ((to["x"] * 4 + to["y"]) * 2 + c) * 4 + to["z"])
                    )
    return pairs


PAIRS = {(axis, near): exchange_pairs(axis, near) for axis in "xyz" for near in (True, False)}


def unit(values):
    squares = jnp.sum(values * values, axis=0, keepdims=True)
    return values * lax.rsqrt(squares + epsilon)


def pack_kernel(query_ref, ids_ref, out_ref):
    out_ref[0, 16:, :] = unit(query_ref[0].astype(f32)).T.astype(bf16)
    ids = ids_ref[...]
    high = lax.shift_right_logical(ids, 6).astype(f32)
    low = (ids & 63).astype(f32)
    row = jnp.concatenate([high, low], axis=1)
    first = lax.broadcasted_iota(jnp.int32, (16, 2 * CAND), 0) == 0
    out_ref[0, :16, :] = jnp.where(first, jnp.broadcast_to(row, first.shape), 0.0).astype(bf16)


def pack(query_maps, shortlist):
    return pl.pallas_call(
        pack_kernel,
        out_shape=jax.ShapeDtypeStruct((1, CELLS + 16, CELLS), bf16),
    )(query_maps, shortlist)


def images_kernel(tap_q_ref, tap_d_ref, maps_ref, unit_ref, conv_q_ref, conv_d_ref):
    for image in range(maps_ref.shape[0]):
        unit_ref[image] = unit(maps_ref[image].astype(f32)).astype(bf16)

    @pl.when(pl.program_id(0) == 0)
    def _():
        near = lax.broadcasted_iota(jnp.int32, (CELLS, CELLS), 0)
        far = lax.broadcasted_iota(jnp.int32, (CELLS, CELLS), 1)
        for tap_ref, out_ref, result, source in (
            (tap_q_ref, conv_q_ref, near, far),
            (tap_d_ref, conv_d_ref, far, near),
        ):
            down = lax.shift_right_logical(source, 4) - lax.shift_right_logical(result, 4)
            right = (source & (GRID - 1)) - (result & (GRID - 1))
            matrix = jnp.zeros((CELLS, CELLS), f32)
            taps = tap_ref[...].astype(f32)
            for i in range(3):
                for j in range(3):
                    hit = (down == i - 1) & (right == j - 1)
                    matrix = jnp.where(hit, taps[i : i + 1, j : j + 1], matrix)
            out_ref[...] = matrix.astype(bf16)


def prepare_images(database, tap_q, tap_d):
    block = 4
    maps = pl.BlockSpec((block, CELLS, CELLS), lambda i: (i, 0, 0))
    square = pl.BlockSpec((CELLS, CELLS), lambda i: (0, 0))
    taps = pl.BlockSpec((3, 3), lambda i: (0, 0))
    square_shape = jax.ShapeDtypeStruct((CELLS, CELLS), bf16)
    return pl.pallas_call(
        images_kernel,
        grid=(database.shape[0] // block,),
        in_specs=[taps, taps, maps],
        out_specs=(maps, square, square),
        out_shape=(jax.ShapeDtypeStruct(database.shape, bf16), square_shape, square_shape),
    )(tap_q, tap_d, database)


def move(array, step):
    return lax.ppermute(array, MAIN, PAIRS[step])


def spread(held):
    pieces = []
    for piece in range(3):
        first = CUTS[piece] + (16 if piece else 0)
        pieces.append(held[:, first : CUTS[piece + 1] + 16])
    order = [(LATE[piece % 3], LATE[(piece + 1) % 3], LATE[(piece + 2) % 3]) for piece in (0, 2, 1)]
    came = [move(p, o[0]) for p, o in zip(pieces, order)]
    pieces = [jnp.concatenate(pair, axis=0) for pair in zip(pieces, came)]
    second = [move(p, o[1]) for p, o in zip(pieces, order)]
    third = [move(p, o[2]) for p, o in zip(pieces, order)]
    fourth = [move(p, o[2]) for p, o in zip(second, order)]
    return [list(part) for part in zip(pieces, second, third, fourth)]


def pair_kernel(
    place_ref, *refs,
):
    parts, refs = refs[:12], refs[12:]
    own_hbm, other_hbm, conv_q_ref, conv_d_ref, out_ref = refs[:5]
    query_v, image_v, ids_v, table_v, column_v, peak_v, total_v, table_s, pair_s, sems = refs[5:]
    id_copies, copies = [], []
    for combo in range(8):
        bits = (combo & 1, combo >> 1 & 1, combo >> 2)
        here = pl.ds(GROUP * combo, GROUP)
        for piece, turn in enumerate((0, 2, 1)):
            source = parts[4 * piece + bits[(turn + 1) % 3] + 2 * bits[(turn + 2) % 3]]
            blocks = pl.ds(GROUP * bits[turn], GROUP)
            size = CUTS[piece + 1] - CUTS[piece]
            skip = 0 if piece else 16
            copies.append(
                pltpu.make_async_copy(
                    source.at[blocks, pl.ds(skip, size), :],
                    query_v.at[here, pl.ds(CUTS[piece], size), :],
                    sems.at[1],
                )
            )
            if piece == 0:
                id_copies.append(
                    pltpu.make_async_copy(
                        source.at[blocks, pl.ds(0, 16), :], ids_v.at[here], sems.at[0]
                    )
                )
    image_copies = [
        pltpu.make_async_copy(own_hbm, image_v.at[pl.ds(0, IMAGES)], sems.at[2]),
        pltpu.make_async_copy(other_hbm, image_v.at[pl.ds(IMAGES, IMAGES)], sems.at[3]),
    ]
    for copy in id_copies + image_copies + copies:
        copy.start()
    pltpu.make_async_copy(ids_v, ids_v, sems.at[0]).wait()
    packed = jnp.sum(ids_v[...].astype(f32), axis=1)
    ids = packed[:, :CAND].astype(jnp.int32) * 64 + packed[:, CAND:].astype(jnp.int32)
    lane = lax.broadcasted_iota(jnp.int32, (NODES, CAND), 1)
    shard = lax.shift_right_logical(ids, 5)
    slot = ids & (IMAGES - 1)
    table = jnp.full((NODES, CAND), -1, jnp.int32)
    for side in range(2):
        held = shard == place_ref[side]
        first = jnp.min(jnp.where(held, lane, CAND), axis=1, keepdims=True)
        last = jnp.max(jnp.where(held, lane, -1), axis=1, keepdims=True)
        last = jnp.where(last > first, last, -1)
        for which, column in ((2 * side, first), (2 * side + 1, last)):
            at = lane == column
            image = jnp.max(jnp.where(at, slot, -1), axis=1, keepdims=True)
            image = jnp.where(image >= 0, image + side * IMAGES, -1)
            table = jnp.where(lane == which, image, table)
            column_v[which] = jnp.broadcast_to(column, (NODES, CAND))
    table_v[...] = table
    move = pltpu.make_async_copy(table_v, table_s, sems.at[4])
    move.start()
    move.wait()

    def fill(query, count):
        for which in range(4):
            image = table_s[query, which]
            pair_s[count] = query * 65536 + (which * NODES + query) * 64 + jnp.maximum(image, 0)
            count = count + (image >= 0).astype(jnp.int32)
        return count

    count = lax.fori_loop(0, NODES, fill, jnp.int32(0))
    for extra in range(UNROLL):
        pair_s[count + extra] = SPARE * 64
    for copy in image_copies:
        copy.wait()
    pltpu.make_async_copy(query_v, query_v, sems.at[1]).wait()

    def group(step, carry):
        found = []
        for part in range(UNROLL):
            code = pair_s[step * UNROLL + part]
            node = lax.shift_right_logical(code, 16)
            image = code & 63
            correlation = jnp.dot(query_v[node], image_v[image], preferred_element_type=f32)
            rectified = jnp.maximum(correlation, 0.0).astype(bf16)
            found.append((lax.shift_right_logical(code, 6) & 1023, rectified))
        for row, rectified in found:
            filtered = jnp.dot(conv_q_ref[...], rectified, preferred_element_type=f32)
            filtered = filtered + jnp.dot(rectified, conv_d_ref[...], preferred_element_type=f32)
            peak_v[pl.ds(row, 1), :] = jnp.max(filtered, axis=0, keepdims=True)
        return carry

    lax.fori_loop(0, (count + UNROLL - 1) // UNROLL, group, 0)
    total = jnp.zeros((NODES, CAND), f32)
    for which in range(4):
        peaks = peak_v[pl.ds(which * NODES, NODES), :]
        score = jnp.sum(peaks, axis=1, keepdims=True) * (score_scale / CELLS)
        total = jnp.where(lane == column_v[which], score, total)
    total_v[...] = total

    def settle(query, carry):
        out_ref[pl.ds(place_ref[2 + query], 1), :] = total_v[pl.ds(query, 1), :]
        return carry

    lax.fori_loop(0, NODES, settle, 0, unroll=8)


def pair_scores(place, parts, own, other, conv_q, conv_d):
    smem = pl.BlockSpec(memory_space=pltpu.SMEM)
    vmem = pl.BlockSpec(memory_space=pltpu.VMEM)
    hbm = pl.BlockSpec(memory_space=pl.ANY)
    return pl.pallas_call(
        pair_kernel,
        out_shape=jax.ShapeDtypeStruct((NODES, CAND), f32),
        in_specs=[smem] + [hbm] * 14 + [vmem, vmem],
        out_specs=vmem,
        scratch_shapes=[
            pltpu.VMEM((NODES, CELLS, CELLS), bf16),
            pltpu.VMEM((2 * IMAGES, CELLS, CELLS), bf16),
            pltpu.VMEM((NODES, 16, CELLS), bf16),
            pltpu.VMEM((NODES, CAND), jnp.int32),
            pltpu.VMEM((4, NODES, CAND), jnp.int32),
            pltpu.VMEM((4 * NODES + 8, CELLS), f32),
            pltpu.VMEM((NODES, CAND), f32),
            pltpu.SMEM((NODES, CAND), jnp.int32),
            pltpu.SMEM((4 * NODES + UNROLL,), jnp.int32),
            pltpu.SemaphoreType.DMA((5,)),
        ],
        compiler_params=pltpu.CompilerParams(vmem_limit_bytes=48 * 2**20),
    )(place, *parts, own, other, conv_q, conv_d)


def finish_kernel(parts_ref, scores_ref, top_ref):
    row = jnp.sum(parts_ref[...], axis=0, keepdims=True)
    scores_ref[...] = row
    across = jnp.broadcast_to(row, (CAND, CAND))
    down = across.T
    at_row = lax.broadcasted_iota(jnp.int32, (CAND, CAND), 0)
    at_col = lax.broadcasted_iota(jnp.int32, (CAND, CAND), 1)
    ahead = (across > down) | ((across == down) & (at_col < at_row))
    rank = jnp.sum(ahead.astype(f32), axis=1, keepdims=True)
    placed = jnp.where(rank == at_col.astype(f32), down, 0.0)
    top_ref[...] = jnp.sum(placed, axis=0, keepdims=True)[:, :TOPK]


def finish(parts):
    return pl.pallas_call(
        finish_kernel,
        out_shape=(
            jax.ShapeDtypeStruct((1, CAND), f32),
            jax.ShapeDtypeStruct((1, TOPK), f32),
        ),
    )(parts)


def place_table():
    me = lax.axis_index("c")
    x, y, z = [lax.axis_index(axis) for axis in NODE]
    base = (x * 4 + y) * 8 + z
    near = jnp.where(me == 0, 1, 3)
    far = 4 - near
    index = jnp.arange(NODES, dtype=jnp.int32)
    bit = [lax.shift_right_logical(index, k) & 1 for k in range(6)]
    z = z ^ (bit[0] * near) ^ (bit[4] * far)
    x = x ^ (bit[1] * near) ^ (bit[5] * far)
    y = y ^ (bit[2] * far) ^ (bit[3] * near)
    shards = jnp.stack([base + 4 * me, base + 4 * (1 - me)])
    return jnp.concatenate([shards, (x * 4 + y) * 4 + z]).astype(jnp.int32)


def body(query_maps, database, shortlist, kernel_query, kernel_db):
    held = pack(query_maps, shortlist)
    for count, step in enumerate(WHOLE):
        held = jnp.concatenate([held, move(held, step)], axis=0)
        if count == 1:
            database, held = lax.optimization_barrier((database, held))
    own, conv_q, conv_d = prepare_images(database, kernel_query, kernel_db)
    other = lax.ppermute(own, "c", [(0, 1), (1, 0)])
    parts = [p for part in spread(held) for p in part]
    scores = pair_scores(place_table(), parts, own, other, conv_q, conv_d)
    scores = lax.all_to_all(scores, NODE, split_axis=0, concat_axis=0, tiled=True)
    return finish(scores)


def solution(mesh):
    fine = Mesh(mesh.devices.reshape(4, 4, 2, 4), MAIN)
    in_specs = (P(MAIN, None, None), P(MAIN, None, None), P(MAIN, None), P(), P())
    out_specs = (P(MAIN, None), P(MAIN, None))
    return jax.shard_map(body, mesh=fine, in_specs=in_specs, out_specs=out_specs, check_vma=False)
```

```python
import functools

import jax
import jax.numpy as jnp
from jax import lax
from jax.experimental import pallas as pl
from jax.experimental.pallas import tpu as pltpu
from jax.sharding import Mesh, PartitionSpec as P

GRID = 16
CELLS = GRID * GRID
TOPK = 100
CAND = 128
IMAGES = 32
NODES = 64
CUTS = (0, 80, 176, CELLS)
UNROLL = 8

epsilon = 1e-06
score_scale = 8.0
f32 = jnp.float32
bf16 = jnp.bfloat16

MAIN = ("x", "y", "c", "z")
NODE = ("x", "y", "z")
WHOLE = (("z", True), ("x", True), ("y", False))
LATE = (("y", True), ("z", False), ("x", False))
GROUP = 8
WAVES = ((0,), (1, 2, 4), (3, 5, 6, 7))


def exchange_pairs(axis, near):
    pairs = []
    for x in range(4):
        for y in range(4):
            for c in range(2):
                for z in range(4):
                    at = {"x": x, "y": y, "z": z}
                    to = dict(at)
                    to[axis] = at[axis] ^ (1 if (c == 0) == near else 3)
                    pairs.append(
                        (((x * 4 + y) * 2 + c) * 4 + z, ((to["x"] * 4 + to["y"]) * 2 + c) * 4 + to["z"])
                    )
    return pairs


PAIRS = {(axis, near): exchange_pairs(axis, near) for axis in "xyz" for near in (True, False)}


def unit(values):
    squares = jnp.sum(values * values, axis=0, keepdims=True)
    return values * lax.rsqrt(squares + epsilon)


def pack_kernel(query_ref, ids_ref, out_ref):
    out_ref[0, 16:, :] = unit(query_ref[0].astype(f32)).T.astype(bf16)
    ids = ids_ref[...]
    high = lax.shift_right_logical(ids, 6).astype(f32)
    low = (ids & 63).astype(f32)
    row = jnp.concatenate([high, low], axis=1)
    first = lax.broadcasted_iota(jnp.int32, (16, 2 * CAND), 0) == 0
    out_ref[0, :16, :] = jnp.where(first, jnp.broadcast_to(row, first.shape), 0.0).astype(bf16)


def pack(query_maps, shortlist):
    return pl.pallas_call(
        pack_kernel,
        out_shape=jax.ShapeDtypeStruct((1, CELLS + 16, CELLS), bf16),
    )(query_maps, shortlist)


def images_kernel(tap_q_ref, tap_d_ref, maps_ref, unit_ref, conv_q_ref, conv_d_ref):
    for image in range(maps_ref.shape[0]):
        unit_ref[image] = unit(maps_ref[image].astype(f32)).astype(bf16)

    @pl.when(pl.program_id(0) == 0)
    def _():
        near = lax.broadcasted_iota(jnp.int32, (CELLS, CELLS), 0)
        far = lax.broadcasted_iota(jnp.int32, (CELLS, CELLS), 1)
        for tap_ref, out_ref, result, source in (
            (tap_q_ref, conv_q_ref, near, far),
            (tap_d_ref, conv_d_ref, far, near),
        ):
            down = lax.shift_right_logical(source, 4) - lax.shift_right_logical(result, 4)
            right = (source & (GRID - 1)) - (result & (GRID - 1))
            matrix = jnp.zeros((CELLS, CELLS), f32)
            taps = tap_ref[...].astype(f32)
            for i in range(3):
                for j in range(3):
                    hit = (down == i - 1) & (right == j - 1)
                    matrix = jnp.where(hit, taps[i : i + 1, j : j + 1], matrix)
            out_ref[...] = matrix.astype(bf16)


def prepare_images(database, tap_q, tap_d):
    block = 4
    maps = pl.BlockSpec((block, CELLS, CELLS), lambda i: (i, 0, 0))
    square = pl.BlockSpec((CELLS, CELLS), lambda i: (0, 0))
    taps = pl.BlockSpec((3, 3), lambda i: (0, 0))
    square_shape = jax.ShapeDtypeStruct((CELLS, CELLS), bf16)
    return pl.pallas_call(
        images_kernel,
        grid=(database.shape[0] // block,),
        in_specs=[taps, taps, maps],
        out_specs=(maps, square, square),
        out_shape=(jax.ShapeDtypeStruct(database.shape, bf16), square_shape, square_shape),
        cost_estimate=pl.CostEstimate(flops=2**24, bytes_accessed=20 * 2**20, transcendentals=0),
    )(tap_q, tap_d, database)


def move(array, step):
    return lax.ppermute(array, MAIN, PAIRS[step])


def spread(held):
    pieces = []
    for piece in range(3):
        first = CUTS[piece] + (16 if piece else 0)
        pieces.append(held[:, first : CUTS[piece + 1] + 16])
    order = [(LATE[piece % 3], LATE[(piece + 1) % 3], LATE[(piece + 2) % 3]) for piece in (0, 2, 1)]
    came = [move(p, o[0]) for p, o in zip(pieces, order)]
    pieces = [jnp.concatenate(pair, axis=0) for pair in zip(pieces, came)]
    second = [move(p, o[1]) for p, o in zip(pieces, order)]
    third = [move(p, o[2]) for p, o in zip(pieces, order)]
    fourth = [move(p, o[2]) for p, o in zip(second, order)]
    return [list(part) for part in zip(pieces, second, third, fourth)]


def sources(combo):
    bits = (combo & 1, combo >> 1 & 1, combo >> 2)
    for turn in (0, 2, 1):
        yield bits[(turn + 1) % 3] + 2 * bits[(turn + 2) % 3], bits[turn]


def pair_kernel(wave, names, place_ref, *refs):
    held = len(WAVES[wave]) * GROUP
    spare = 4 * held
    parts, refs = dict(zip(names, refs)), refs[len(names) :]
    earlier = ()
    if wave == 2:
        earlier, refs = refs[:2], refs[2:]
    own_hbm, other_hbm, conv_q_ref, conv_d_ref, out_ref = refs[:5]
    query_v, image_v, ids_v, table_v, column_v, peak_v, total_v, table_s, pair_s, sems = refs[5:]
    id_copies, copies = [], []
    for local, combo in enumerate(WAVES[wave]):
        here = pl.ds(GROUP * local, GROUP)
        for piece, (which, half) in enumerate(sources(combo)):
            source = parts[piece, which]
            blocks = pl.ds(GROUP * half, GROUP)
            size = CUTS[piece + 1] - CUTS[piece]
            skip = 0 if piece else 16
            copies.append(
                pltpu.make_async_copy(
                    source.at[blocks, pl.ds(skip, size), :],
                    query_v.at[here, pl.ds(CUTS[piece], size), :],
                    sems.at[1],
                )
            )
            if piece == 0:
                id_copies.append(
                    pltpu.make_async_copy(
                        source.at[blocks, pl.ds(0, 16), :], ids_v.at[here], sems.at[0]
                    )
                )
    image_copies = [
        pltpu.make_async_copy(own_hbm, image_v.at[pl.ds(0, IMAGES)], sems.at[2]),
        pltpu.make_async_copy(other_hbm, image_v.at[pl.ds(IMAGES, IMAGES)], sems.at[3]),
    ]
    for copy in id_copies + image_copies + copies:
        copy.start()
    pltpu.make_async_copy(ids_v, ids_v, sems.at[0]).wait()
    packed = jnp.sum(ids_v[...].astype(f32), axis=1)
    ids = packed[:, :CAND].astype(jnp.int32) * 64 + packed[:, CAND:].astype(jnp.int32)
    lane = lax.broadcasted_iota(jnp.int32, (held, CAND), 1)
    shard = lax.shift_right_logical(ids, 5)
    slot = ids & (IMAGES - 1)
    table = jnp.full((held, CAND), -1, jnp.int32)
    for side in range(2):
        mine = shard == place_ref[side]
        first = jnp.min(jnp.where(mine, lane, CAND), axis=1, keepdims=True)
        last = jnp.max(jnp.where(mine, lane, -1), axis=1, keepdims=True)
        last = jnp.where(last > first, last, -1)
        for which, column in ((2 * side, first), (2 * side + 1, last)):
            at = lane == column
            image = jnp.max(jnp.where(at, slot, -1), axis=1, keepdims=True)
            image = jnp.where(image >= 0, image + side * IMAGES, -1)
            table = jnp.where(lane == which, image, table)
            column_v[which] = jnp.broadcast_to(column, (held, CAND))
    table_v[...] = table
    move = pltpu.make_async_copy(table_v, table_s, sems.at[4])
    move.start()
    move.wait()

    def fill(query, count):
        for which in range(4):
            image = table_s[query, which]
            pair_s[count] = query * 65536 + (which * held + query) * 64 + jnp.maximum(image, 0)
            count = count + (image >= 0).astype(jnp.int32)
        return count

    count = lax.fori_loop(0, held, fill, jnp.int32(0))
    for extra in range(UNROLL):
        pair_s[count + extra] = spare * 64
    for copy in image_copies:
        copy.wait()
    pltpu.make_async_copy(query_v, query_v, sems.at[1]).wait()

    def group(step, carry):
        found = []
        for part in range(UNROLL):
            code = pair_s[step * UNROLL + part]
            node = lax.shift_right_logical(code, 16)
            image = code & 63
            correlation = jnp.dot(query_v[node], image_v[image], preferred_element_type=f32)
            rectified = jnp.maximum(correlation, 0.0).astype(bf16)
            found.append((lax.shift_right_logical(code, 6) & 1023, rectified))
        for row, rectified in found:
            filtered = jnp.dot(conv_q_ref[...], rectified, preferred_element_type=f32)
            filtered = filtered + jnp.dot(rectified, conv_d_ref[...], preferred_element_type=f32)
            peak_v[pl.ds(row, 1), :] = jnp.max(filtered, axis=0, keepdims=True)
        return carry

    lax.fori_loop(0, (count + UNROLL - 1) // UNROLL, group, 0)
    total = jnp.zeros((held, CAND), f32)
    for which in range(4):
        peaks = peak_v[pl.ds(which * held, held), :]
        score = jnp.sum(peaks, axis=1, keepdims=True) * (score_scale / CELLS)
        total = jnp.where(lane == column_v[which], score, total)
    if wave < 2:
        out_ref[...] = total
        return
    done = 0
    for ref in earlier:
        total_v[pl.ds(done, ref.shape[0]), :] = ref[...]
        done += ref.shape[0]
    total_v[pl.ds(done, held), :] = total

    def settle(query, carry):
        out_ref[pl.ds(place_ref[2 + query], 1), :] = total_v[pl.ds(query, 1), :]
        return carry

    lax.fori_loop(0, NODES, settle, 0, unroll=8)


def pair_scores(wave, place, parts, earlier, own, other, conv_q, conv_d):
    smem = pl.BlockSpec(memory_space=pltpu.SMEM)
    vmem = pl.BlockSpec(memory_space=pltpu.VMEM)
    hbm = pl.BlockSpec(memory_space=pl.ANY)
    held = len(WAVES[wave]) * GROUP
    names = sorted(
        {(piece, which) for combo in WAVES[wave] for piece, (which, _) in enumerate(sources(combo))}
    )
    return pl.pallas_call(
        functools.partial(pair_kernel, wave, names),
        out_shape=jax.ShapeDtypeStruct((NODES if wave == 2 else held, CAND), f32),
        in_specs=[smem] + [hbm] * len(names) + [vmem] * len(earlier) + [hbm, hbm, vmem, vmem],
        out_specs=vmem,
        scratch_shapes=[
            pltpu.VMEM((held, CELLS, CELLS), bf16),
            pltpu.VMEM((2 * IMAGES, CELLS, CELLS), bf16),
            pltpu.VMEM((held, 16, CELLS), bf16),
            pltpu.VMEM((held, CAND), jnp.int32),
            pltpu.VMEM((4, held, CAND), jnp.int32),
            pltpu.VMEM((4 * held + 8, CELLS), f32),
            pltpu.VMEM((NODES, CAND), f32),
            pltpu.SMEM((held, CAND), jnp.int32),
            pltpu.SMEM((4 * held + UNROLL,), jnp.int32),
            pltpu.SemaphoreType.DMA((5,)),
        ],
        compiler_params=pltpu.CompilerParams(vmem_limit_bytes=28 * 2**20),
        cost_estimate=pl.CostEstimate(
            flops=3 * held * 6 * CELLS**3, bytes_accessed=16 * 2**20, transcendentals=0
        ),
    )(place, *[parts[piece][which] for piece, which in names], *earlier, own, other, conv_q, conv_d)


def finish_kernel(parts_ref, scores_ref, top_ref):
    row = jnp.sum(parts_ref[...], axis=0, keepdims=True)
    scores_ref[...] = row
    across = jnp.broadcast_to(row, (CAND, CAND))
    down = across.T
    at_row = lax.broadcasted_iota(jnp.int32, (CAND, CAND), 0)
    at_col = lax.broadcasted_iota(jnp.int32, (CAND, CAND), 1)
    ahead = (across > down) | ((across == down) & (at_col < at_row))
    rank = jnp.sum(ahead.astype(f32), axis=1, keepdims=True)
    placed = jnp.where(rank == at_col.astype(f32), down, 0.0)
    top_ref[...] = jnp.sum(placed, axis=0, keepdims=True)[:, :TOPK]


def finish(parts):
    return pl.pallas_call(
        finish_kernel,
        out_shape=(
            jax.ShapeDtypeStruct((1, CAND), f32),
            jax.ShapeDtypeStruct((1, TOPK), f32),
        ),
    )(parts)


def place_table():
    me = lax.axis_index("c")
    x, y, z = [lax.axis_index(axis) for axis in NODE]
    base = (x * 4 + y) * 8 + z
    near = jnp.where(me == 0, 1, 3)
    far = 4 - near
    combos = jnp.array([combo for wave in WAVES for combo in wave], jnp.int32)
    index = (combos[:, None] * GROUP + jnp.arange(GROUP, dtype=jnp.int32)).reshape(-1)
    bit = [lax.shift_right_logical(index, k) & 1 for k in range(6)]
    z = z ^ (bit[0] * near) ^ (bit[4] * far)
    x = x ^ (bit[1] * near) ^ (bit[5] * far)
    y = y ^ (bit[2] * far) ^ (bit[3] * near)
    shards = jnp.stack([base + 4 * me, base + 4 * (1 - me)])
    return jnp.concatenate([shards, (x * 4 + y) * 4 + z]).astype(jnp.int32)


def body(query_maps, database, shortlist, kernel_query, kernel_db):
    held = pack(query_maps, shortlist)
    for count, step in enumerate(WHOLE):
        held = jnp.concatenate([held, move(held, step)], axis=0)
        if count == 1:
            database, held = lax.optimization_barrier((database, held))
    own, conv_q, conv_d = prepare_images(database, kernel_query, kernel_db)
    other = lax.ppermute(own, "c", [(0, 1), (1, 0)])
    parts = spread(held)
    place = place_table()
    first = pair_scores(0, place, parts, (), own, other, conv_q, conv_d)
    second = pair_scores(1, place, parts, (), own, other, conv_q, conv_d)
    scores = pair_scores(2, place, parts, (first, second), own, other, conv_q, conv_d)
    scores = lax.all_to_all(scores, NODE, split_axis=0, concat_axis=0, tiled=True)
    return finish(scores)


def solution(mesh):
    fine = Mesh(mesh.devices.reshape(4, 4, 2, 4), MAIN)
    in_specs = (P(MAIN, None, None), P(MAIN, None, None), P(MAIN, None), P(), P())
    out_specs = (P(MAIN, None), P(MAIN, None))
    return jax.shard_map(body, mesh=fine, in_specs=in_specs, out_specs=out_specs, check_vma=False)
```

```python
import functools

import jax
import jax.numpy as jnp
from jax import lax
from jax.experimental import pallas as pl
from jax.experimental.pallas import tpu as pltpu
from jax.sharding import Mesh, PartitionSpec as P

GRID = 16
CELLS = GRID * GRID
TOPK = 100
CAND = 128
IMAGES = 32
NODES = 64
CUTS = (0, 80, 176, CELLS)
UNROLL = 8

epsilon = 1e-06
score_scale = 8.0
f32 = jnp.float32
bf16 = jnp.bfloat16

MAIN = ("x", "y", "c", "z")
NODE = ("x", "y", "z")
WHOLE = (("z", True), ("x", True), ("y", False))
LATE = (("y", True), ("z", False), ("x", False))
GROUP = 8
WAVES = ((0,), (1, 2, 4), (3, 5, 6, 7))


def exchange_pairs(axis, near):
    pairs = []
    for x in range(4):
        for y in range(4):
            for c in range(2):
                for z in range(4):
                    at = {"x": x, "y": y, "z": z}
                    to = dict(at)
                    to[axis] = at[axis] ^ (1 if (c == 0) == near else 3)
                    pairs.append(
                        (((x * 4 + y) * 2 + c) * 4 + z, ((to["x"] * 4 + to["y"]) * 2 + c) * 4 + to["z"])
                    )
    return pairs


PAIRS = {(axis, near): exchange_pairs(axis, near) for axis in "xyz" for near in (True, False)}


def unit(values):
    squares = jnp.sum(values * values, axis=0, keepdims=True)
    return values * lax.rsqrt(squares + epsilon)


def pack_kernel(query_ref, ids_ref, out_ref):
    out_ref[0, 16:, :] = unit(query_ref[0].astype(f32)).T.astype(bf16)
    ids = ids_ref[...]
    high = lax.shift_right_logical(ids, 6).astype(f32)
    low = (ids & 63).astype(f32)
    row = jnp.concatenate([high, low], axis=1)
    first = lax.broadcasted_iota(jnp.int32, (16, 2 * CAND), 0) == 0
    out_ref[0, :16, :] = jnp.where(first, jnp.broadcast_to(row, first.shape), 0.0).astype(bf16)


def pack(query_maps, shortlist):
    return pl.pallas_call(
        pack_kernel,
        out_shape=jax.ShapeDtypeStruct((1, CELLS + 16, CELLS), bf16),
    )(query_maps, shortlist)


def images_kernel(tap_q_ref, tap_d_ref, maps_ref, unit_ref, conv_q_ref, conv_d_ref):
    for image in range(maps_ref.shape[0]):
        unit_ref[image] = unit(maps_ref[image].astype(f32)).astype(bf16)

    @pl.when(pl.program_id(0) == 0)
    def _():
        near = lax.broadcasted_iota(jnp.int32, (CELLS, CELLS), 0)
        far = lax.broadcasted_iota(jnp.int32, (CELLS, CELLS), 1)
        for tap_ref, out_ref, result, source in (
            (tap_q_ref, conv_q_ref, near, far),
            (tap_d_ref, conv_d_ref, far, near),
        ):
            down = lax.shift_right_logical(source, 4) - lax.shift_right_logical(result, 4)
            right = (source & (GRID - 1)) - (result & (GRID - 1))
            matrix = jnp.zeros((CELLS, CELLS), f32)
            taps = tap_ref[...].astype(f32)
            for i in range(3):
                for j in range(3):
                    hit = (down == i - 1) & (right == j - 1)
                    matrix = jnp.where(hit, taps[i : i + 1, j : j + 1], matrix)
            out_ref[...] = matrix.astype(bf16)


def prepare_images(database, tap_q, tap_d):
    block = 4
    maps = pl.BlockSpec((block, CELLS, CELLS), lambda i: (i, 0, 0))
    square = pl.BlockSpec((CELLS, CELLS), lambda i: (0, 0))
    taps = pl.BlockSpec((3, 3), lambda i: (0, 0))
    square_shape = jax.ShapeDtypeStruct((CELLS, CELLS), bf16)
    return pl.pallas_call(
        images_kernel,
        grid=(database.shape[0] // block,),
        in_specs=[taps, taps, maps],
        out_specs=(maps, square, square),
        out_shape=(jax.ShapeDtypeStruct(database.shape, bf16), square_shape, square_shape),
        cost_estimate=pl.CostEstimate(flops=2**24, bytes_accessed=20 * 2**20, transcendentals=0),
    )(tap_q, tap_d, database)


def move(array, step):
    return lax.ppermute(array, MAIN, PAIRS[step])


def spread(held):
    pieces = []
    for piece in range(3):
        first = CUTS[piece] + (16 if piece else 0)
        pieces.append(held[:, first : CUTS[piece + 1] + 16])
    order = [(LATE[piece % 3], LATE[(piece + 1) % 3], LATE[(piece + 2) % 3]) for piece in (0, 2, 1)]
    came = [move(p, o[0]) for p, o in zip(pieces, order)]
    pieces = [jnp.concatenate(pair, axis=0) for pair in zip(pieces, came)]
    second = [move(p, o[1]) for p, o in zip(pieces, order)]
    third = [move(p, o[2]) for p, o in zip(pieces, order)]
    fourth = [move(p, o[2]) for p, o in zip(second, order)]
    return [list(part) for part in zip(pieces, second, third, fourth)]


def sources(combo):
    bits = (combo & 1, combo >> 1 & 1, combo >> 2)
    for turn in (0, 2, 1):
        yield bits[(turn + 1) % 3] + 2 * bits[(turn + 2) % 3], bits[turn]


def pair_kernel(wave, names, place_ref, *refs):
    held = len(WAVES[wave]) * GROUP
    spare = 4 * held
    parts, refs = dict(zip(names, refs)), refs[len(names) :]
    earlier = ()
    if wave == 2:
        earlier, refs = refs[:2], refs[2:]
    own_hbm, other_hbm, conv_q_ref, conv_d_ref, out_ref = refs[:5]
    query_v, image_v, ids_v, table_v, column_v, peak_v, total_v, table_s, pair_s, sems = refs[5:]
    id_copies, copies = [], []
    for local, combo in enumerate(WAVES[wave]):
        here = pl.ds(GROUP * local, GROUP)
        for piece, (which, half) in enumerate(sources(combo)):
            source = parts[piece, which]
            blocks = pl.ds(GROUP * half, GROUP)
            size = CUTS[piece + 1] - CUTS[piece]
            skip = 0 if piece else 16
            copies.append(
                pltpu.make_async_copy(
                    source.at[blocks, pl.ds(skip, size), :],
                    query_v.at[here, pl.ds(CUTS[piece], size), :],
                    sems.at[1],
                )
            )
            if piece == 0:
                id_copies.append(
                    pltpu.make_async_copy(
                        source.at[blocks, pl.ds(0, 16), :], ids_v.at[here], sems.at[0]
                    )
                )
    image_copies = [
        pltpu.make_async_copy(own_hbm, image_v.at[pl.ds(0, IMAGES)], sems.at[2]),
        pltpu.make_async_copy(other_hbm, image_v.at[pl.ds(IMAGES, IMAGES)], sems.at[3]),
    ]
    for copy in id_copies + image_copies + copies:
        copy.start()
    pltpu.make_async_copy(ids_v, ids_v, sems.at[0]).wait()
    packed = jnp.sum(ids_v[...].astype(f32), axis=1)
    ids = packed[:, :CAND].astype(jnp.int32) * 64 + packed[:, CAND:].astype(jnp.int32)
    lane = lax.broadcasted_iota(jnp.int32, (held, CAND), 1)
    shard = lax.shift_right_logical(ids, 5)
    slot = ids & (IMAGES - 1)
    table = jnp.full((held, CAND), -1, jnp.int32)
    for side in range(2):
        mine = shard == place_ref[side]
        first = jnp.min(jnp.where(mine, lane, CAND), axis=1, keepdims=True)
        last = jnp.max(jnp.where(mine, lane, -1), axis=1, keepdims=True)
        last = jnp.where(last > first, last, -1)
        for which, column in ((2 * side, first), (2 * side + 1, last)):
            at = lane == column
            image = jnp.max(jnp.where(at, slot, -1), axis=1, keepdims=True)
            image = jnp.where(image >= 0, image + side * IMAGES, -1)
            table = jnp.where(lane == which, image, table)
            column_v[which] = jnp.broadcast_to(column, (held, CAND))
    table_v[...] = table
    move = pltpu.make_async_copy(table_v, table_s, sems.at[4])
    move.start()
    move.wait()

    def fill(query, count):
        for which in range(4):
            image = table_s[query, which]
            pair_s[count] = query * 65536 + (which * held + query) * 64 + jnp.maximum(image, 0)
            count = count + (image >= 0).astype(jnp.int32)
        return count

    count = lax.fori_loop(0, held, fill, jnp.int32(0))
    for extra in range(UNROLL):
        pair_s[count + extra] = spare * 64
    for copy in image_copies:
        copy.wait()
    pltpu.make_async_copy(query_v, query_v, sems.at[1]).wait()

    def group(step, carry):
        found = []
        for part in range(UNROLL):
            code = pair_s[step * UNROLL + part]
            node = lax.shift_right_logical(code, 16)
            image = code & 63
            correlation = jnp.dot(query_v[node], image_v[image], preferred_element_type=f32)
            rectified = jnp.maximum(correlation, 0.0).astype(bf16)
            found.append((lax.shift_right_logical(code, 6) & 1023, rectified))
        for row, rectified in found:
            filtered = jnp.dot(conv_q_ref[...], rectified, preferred_element_type=f32)
            filtered = filtered + jnp.dot(rectified, conv_d_ref[...], preferred_element_type=f32)
            peak_v[pl.ds(row, 1), :] = jnp.max(filtered, axis=0, keepdims=True)
        return carry

    lax.fori_loop(0, (count + UNROLL - 1) // UNROLL, group, 0)
    total = jnp.zeros((held, CAND), f32)
    for which in range(4):
        peaks = peak_v[pl.ds(which * held, held), :]
        score = jnp.sum(peaks, axis=1, keepdims=True) * (score_scale / CELLS)
        total = jnp.where(lane == column_v[which], score, total)
    if wave < 2:
        out_ref[...] = total
        return
    done = 0
    for ref in earlier:
        total_v[pl.ds(done, ref.shape[0]), :] = ref[...]
        done += ref.shape[0]
    total_v[pl.ds(done, held), :] = total

    def settle(query, carry):
        out_ref[pl.ds(place_ref[2 + query], 1), :] = total_v[pl.ds(query, 1), :]
        return carry

    lax.fori_loop(0, NODES, settle, 0, unroll=8)


def pair_scores(wave, place, parts, earlier, own, other, conv_q, conv_d):
    smem = pl.BlockSpec(memory_space=pltpu.SMEM)
    vmem = pl.BlockSpec(memory_space=pltpu.VMEM)
    hbm = pl.BlockSpec(memory_space=pl.ANY)
    held = len(WAVES[wave]) * GROUP
    names = sorted(
        {(piece, which) for combo in WAVES[wave] for piece, (which, _) in enumerate(sources(combo))}
    )
    return pl.pallas_call(
        functools.partial(pair_kernel, wave, names),
        out_shape=jax.ShapeDtypeStruct((NODES if wave == 2 else held, CAND), f32),
        in_specs=[smem] + [hbm] * len(names) + [vmem] * len(earlier) + [hbm, hbm, vmem, vmem],
        out_specs=vmem,
        scratch_shapes=[
            pltpu.VMEM((held, CELLS, CELLS), bf16),
            pltpu.VMEM((2 * IMAGES, CELLS, CELLS), bf16),
            pltpu.VMEM((held, 16, CELLS), bf16),
            pltpu.VMEM((held, CAND), jnp.int32),
            pltpu.VMEM((4, held, CAND), jnp.int32),
            pltpu.VMEM((4 * held + 8, CELLS), f32),
            pltpu.VMEM((NODES, CAND), f32),
            pltpu.SMEM((held, CAND), jnp.int32),
            pltpu.SMEM((4 * held + UNROLL,), jnp.int32),
            pltpu.SemaphoreType.DMA((5,)),
        ],
        compiler_params=pltpu.CompilerParams(vmem_limit_bytes=28 * 2**20),
        cost_estimate=pl.CostEstimate(
            flops=3 * held * 6 * CELLS**3, bytes_accessed=16 * 2**20, transcendentals=0
        ),
    )(place, *[parts[piece][which] for piece, which in names], *earlier, own, other, conv_q, conv_d)


def finish_kernel(parts_ref, scores_ref, top_ref):
    row = jnp.sum(parts_ref[...], axis=0, keepdims=True)
    scores_ref[...] = row
    across = jnp.broadcast_to(row, (CAND, CAND))
    down = across.T
    at_row = lax.broadcasted_iota(jnp.int32, (CAND, CAND), 0)
    at_col = lax.broadcasted_iota(jnp.int32, (CAND, CAND), 1)
    ahead = (across > down) | ((across == down) & (at_col < at_row))
    rank = jnp.sum(ahead.astype(f32), axis=1, keepdims=True)
    placed = jnp.where(rank == at_col.astype(f32), down, 0.0)
    top_ref[...] = jnp.sum(placed, axis=0, keepdims=True)[:, :TOPK]


def finish(parts):
    return pl.pallas_call(
        finish_kernel,
        out_shape=(
            jax.ShapeDtypeStruct((1, CAND), f32),
            jax.ShapeDtypeStruct((1, TOPK), f32),
        ),
    )(parts)


def place_table():
    me = lax.axis_index("c")
    x, y, z = [lax.axis_index(axis) for axis in NODE]
    base = (x * 4 + y) * 8 + z
    near = jnp.where(me == 0, 1, 3)
    far = 4 - near
    combos = jnp.array([combo for wave in WAVES for combo in wave], jnp.int32)
    index = (combos[:, None] * GROUP + jnp.arange(GROUP, dtype=jnp.int32)).reshape(-1)
    bit = [lax.shift_right_logical(index, k) & 1 for k in range(6)]
    z = z ^ (bit[0] * near) ^ (bit[4] * far)
    x = x ^ (bit[1] * near) ^ (bit[5] * far)
    y = y ^ (bit[2] * far) ^ (bit[3] * near)
    shards = jnp.stack([base + 4 * me, base + 4 * (1 - me)])
    return jnp.concatenate([shards, (x * 4 + y) * 4 + z]).astype(jnp.int32)


def body(query_maps, database, shortlist, kernel_query, kernel_db):
    held = pack(query_maps, shortlist)
    for count, step in enumerate(WHOLE):
        came = move(held, step)
        if count == 2:
            own, conv_q, conv_d = prepare_images(database, kernel_query, kernel_db)
            came, own = lax.optimization_barrier((came, own))
        held = jnp.concatenate([held, came], axis=0)
        if count == 1:
            database, held = lax.optimization_barrier((database, held))
    other = lax.ppermute(own, "c", [(0, 1), (1, 0)])
    parts = spread(held)
    place = place_table()
    first = pair_scores(0, place, parts, (), own, other, conv_q, conv_d)
    second = pair_scores(1, place, parts, (), own, other, conv_q, conv_d)
    scores = pair_scores(2, place, parts, (first, second), own, other, conv_q, conv_d)
    scores = lax.all_to_all(scores, NODE, split_axis=0, concat_axis=0, tiled=True)
    return finish(scores)


def solution(mesh):
    fine = Mesh(mesh.devices.reshape(4, 4, 2, 4), MAIN)
    in_specs = (P(MAIN, None, None), P(MAIN, None, None), P(MAIN, None), P(), P())
    out_specs = (P(MAIN, None), P(MAIN, None))
    return jax.shard_map(body, mesh=fine, in_specs=in_specs, out_specs=out_specs, check_vma=False)
```

```python
import functools

import jax
import jax.numpy as jnp
from jax import lax
from jax.experimental import pallas as pl
from jax.experimental.pallas import tpu as pltpu
from jax.sharding import Mesh, PartitionSpec as P

GRID = 16
CELLS = GRID * GRID
TOPK = 100
CAND = 128
IMAGES = 32
NODES = 64
CUTS = (0, 80, 176, CELLS)
UNROLL = 8

epsilon = 1e-06
score_scale = 8.0
f32 = jnp.float32
bf16 = jnp.bfloat16

MAIN = ("x", "y", "c", "z")
NODE = ("x", "y", "z")
WHOLE = (("z", True), ("x", True), ("y", False))
LATE = (("y", True), ("z", False), ("x", False))
GROUP = 8
WAVES = ((0,), (1, 2, 4), (3, 5, 6, 7))


def exchange_pairs(axis, near):
    pairs = []
    for x in range(4):
        for y in range(4):
            for c in range(2):
                for z in range(4):
                    at = {"x": x, "y": y, "z": z}
                    to = dict(at)
                    to[axis] = at[axis] ^ (1 if (c == 0) == near else 3)
                    pairs.append(
                        (((x * 4 + y) * 2 + c) * 4 + z, ((to["x"] * 4 + to["y"]) * 2 + c) * 4 + to["z"])
                    )
    return pairs


PAIRS = {(axis, near): exchange_pairs(axis, near) for axis in "xyz" for near in (True, False)}


def unit(values):
    squares = jnp.sum(values * values, axis=0, keepdims=True)
    return values * lax.rsqrt(squares + epsilon)


def pack_kernel(query_ref, ids_ref, out_ref):
    out_ref[0, 16:, :] = unit(query_ref[0].astype(f32)).T.astype(bf16)
    ids = ids_ref[...]
    high = lax.shift_right_logical(ids, 6).astype(f32)
    low = (ids & 63).astype(f32)
    row = jnp.concatenate([high, low], axis=1)
    first = lax.broadcasted_iota(jnp.int32, (16, 2 * CAND), 0) == 0
    out_ref[0, :16, :] = jnp.where(first, jnp.broadcast_to(row, first.shape), 0.0).astype(bf16)


def pack(query_maps, shortlist):
    return pl.pallas_call(
        pack_kernel,
        out_shape=jax.ShapeDtypeStruct((1, CELLS + 16, CELLS), bf16),
    )(query_maps, shortlist)


def images_kernel(tap_q_ref, tap_d_ref, maps_ref, unit_ref, conv_q_ref, conv_d_ref):
    for image in range(maps_ref.shape[0]):
        unit_ref[image] = unit(maps_ref[image].astype(f32)).astype(bf16)

    @pl.when(pl.program_id(0) == 0)
    def _():
        near = lax.broadcasted_iota(jnp.int32, (CELLS, CELLS), 0)
        far = lax.broadcasted_iota(jnp.int32, (CELLS, CELLS), 1)
        for tap_ref, out_ref, result, source in (
            (tap_q_ref, conv_q_ref, near, far),
            (tap_d_ref, conv_d_ref, far, near),
        ):
            down = lax.shift_right_logical(source, 4) - lax.shift_right_logical(result, 4)
            right = (source & (GRID - 1)) - (result & (GRID - 1))
            matrix = jnp.zeros((CELLS, CELLS), f32)
            taps = tap_ref[...].astype(f32)
            for i in range(3):
                for j in range(3):
                    hit = (down == i - 1) & (right == j - 1)
                    matrix = jnp.where(hit, taps[i : i + 1, j : j + 1], matrix)
            out_ref[...] = matrix.astype(bf16)


def prepare_images(database, tap_q, tap_d):
    block = 4
    maps = pl.BlockSpec((block, CELLS, CELLS), lambda i: (i, 0, 0))
    square = pl.BlockSpec((CELLS, CELLS), lambda i: (0, 0))
    taps = pl.BlockSpec((3, 3), lambda i: (0, 0))
    square_shape = jax.ShapeDtypeStruct((CELLS, CELLS), bf16)
    return pl.pallas_call(
        images_kernel,
        grid=(database.shape[0] // block,),
        in_specs=[taps, taps, maps],
        out_specs=(maps, square, square),
        out_shape=(jax.ShapeDtypeStruct(database.shape, bf16), square_shape, square_shape),
        cost_estimate=pl.CostEstimate(flops=2**24, bytes_accessed=20 * 2**20, transcendentals=0),
    )(tap_q, tap_d, database)


def move(array, step):
    return lax.ppermute(array, MAIN, PAIRS[step])


def orders():
    return [(LATE[piece % 3], LATE[(piece + 1) % 3], LATE[(piece + 2) % 3]) for piece in (0, 2, 1)]


def split(held):
    pieces = []
    for piece in range(3):
        first = CUTS[piece] + (16 if piece else 0)
        pieces.append(held[:, first : CUTS[piece + 1] + 16])
    came = [move(p, o[0]) for p, o in zip(pieces, orders())]
    return [jnp.concatenate(pair, axis=0) for pair in zip(pieces, came)]


def sources(combo):
    bits = (combo & 1, combo >> 1 & 1, combo >> 2)
    for turn in (0, 2, 1):
        yield bits[(turn + 1) % 3] + 2 * bits[(turn + 2) % 3], bits[turn]


def pair_kernel(wave, names, place_ref, *refs):
    held = len(WAVES[wave]) * GROUP
    spare = 4 * held
    refs, scratch = refs[:-9], refs[-9:]
    query_v, ids_v, table_v, column_v, peak_v, total_v, table_s, pair_s, sems = scratch
    parts, refs = dict(zip(names, refs)), refs[len(names) :]
    earlier = ()
    if wave == 2:
        earlier, refs = refs[:2], refs[2:]
    if wave == 0:
        own_hbm, other_hbm, conv_q_ref, conv_d_ref, out_ref, image_v = refs[:6]
        image_copies = [
            pltpu.make_async_copy(own_hbm, image_v.at[pl.ds(0, IMAGES)], sems.at[2]),
            pltpu.make_async_copy(other_hbm, image_v.at[pl.ds(IMAGES, IMAGES)], sems.at[3]),
        ]
    else:
        image_v, conv_q_ref, conv_d_ref, out_ref = refs[:4]
        image_copies = []
    id_copies, copies = [], []
    for local, combo in enumerate(WAVES[wave]):
        here = pl.ds(GROUP * local, GROUP)
        for piece, (which, half) in enumerate(sources(combo)):
            source = parts[piece, which]
            blocks = pl.ds(GROUP * half, GROUP)
            size = CUTS[piece + 1] - CUTS[piece]
            skip = 0 if piece else 16
            copies.append(
                pltpu.make_async_copy(
                    source.at[blocks, pl.ds(skip, size), :],
                    query_v.at[here, pl.ds(CUTS[piece], size), :],
                    sems.at[1],
                )
            )
            if piece == 0:
                id_copies.append(
                    pltpu.make_async_copy(
                        source.at[blocks, pl.ds(0, 16), :], ids_v.at[here], sems.at[0]
                    )
                )
    for copy in id_copies + image_copies + copies:
        copy.start()
    pltpu.make_async_copy(ids_v, ids_v, sems.at[0]).wait()
    packed = jnp.sum(ids_v[...].astype(f32), axis=1)
    ids = packed[:, :CAND].astype(jnp.int32) * 64 + packed[:, CAND:].astype(jnp.int32)
    lane = lax.broadcasted_iota(jnp.int32, (held, CAND), 1)
    shard = lax.shift_right_logical(ids, 5)
    slot = ids & (IMAGES - 1)
    table = jnp.full((held, CAND), -1, jnp.int32)
    for side in range(2):
        mine = shard == place_ref[side]
        first = jnp.min(jnp.where(mine, lane, CAND), axis=1, keepdims=True)
        last = jnp.max(jnp.where(mine, lane, -1), axis=1, keepdims=True)
        last = jnp.where(last > first, last, -1)
        for which, column in ((2 * side, first), (2 * side + 1, last)):
            at = lane == column
            image = jnp.max(jnp.where(at, slot, -1), axis=1, keepdims=True)
            image = jnp.where(image >= 0, image + side * IMAGES, -1)
            table = jnp.where(lane == which, image, table)
            column_v[which] = jnp.broadcast_to(column, (held, CAND))
    table_v[...] = table
    move = pltpu.make_async_copy(table_v, table_s, sems.at[4])
    move.start()
    move.wait()

    def fill(query, count):
        for which in range(4):
            image = table_s[query, which]
            pair_s[count] = query * 65536 + (which * held + query) * 64 + jnp.maximum(image, 0)
            count = count + (image >= 0).astype(jnp.int32)
        return count

    count = lax.fori_loop(0, held, fill, jnp.int32(0))
    for extra in range(UNROLL):
        pair_s[count + extra] = spare * 64
    for copy in image_copies:
        copy.wait()
    pltpu.make_async_copy(query_v, query_v, sems.at[1]).wait()

    def group(step, carry):
        found = []
        for part in range(UNROLL):
            code = pair_s[step * UNROLL + part]
            node = lax.shift_right_logical(code, 16)
            image = code & 63
            correlation = jnp.dot(query_v[node], image_v[image], preferred_element_type=f32)
            rectified = jnp.maximum(correlation, 0.0).astype(bf16)
            found.append((lax.shift_right_logical(code, 6) & 1023, rectified))
        for row, rectified in found:
            filtered = jnp.dot(conv_q_ref[...], rectified, preferred_element_type=f32)
            filtered = filtered + jnp.dot(rectified, conv_d_ref[...], preferred_element_type=f32)
            peak_v[pl.ds(row, 1), :] = jnp.max(filtered, axis=0, keepdims=True)
        return carry

    lax.fori_loop(0, (count + UNROLL - 1) // UNROLL, group, 0)
    total = jnp.zeros((held, CAND), f32)
    for which in range(4):
        peaks = peak_v[pl.ds(which * held, held), :]
        score = jnp.sum(peaks, axis=1, keepdims=True) * (score_scale / CELLS)
        total = jnp.where(lane == column_v[which], score, total)
    if wave < 2:
        out_ref[...] = total
        return
    done = 0
    for ref in earlier:
        total_v[pl.ds(done, ref.shape[0]), :] = ref[...]
        done += ref.shape[0]
    total_v[pl.ds(done, held), :] = total

    def settle(query, carry):
        out_ref[pl.ds(place_ref[2 + query], 1), :] = total_v[pl.ds(query, 1), :]
        return carry

    lax.fori_loop(0, NODES, settle, 0, unroll=8)


def pair_scores(wave, place, parts, earlier, images, conv_q, conv_d):
    smem = pl.BlockSpec(memory_space=pltpu.SMEM)
    vmem = pl.BlockSpec(memory_space=pltpu.VMEM)
    hbm = pl.BlockSpec(memory_space=pl.ANY)
    held = len(WAVES[wave]) * GROUP
    names = sorted(
        {(piece, which) for combo in WAVES[wave] for piece, (which, _) in enumerate(sources(combo))}
    )
    out_shape = jax.ShapeDtypeStruct((NODES if wave == 2 else held, CAND), f32)
    out_specs = vmem
    image_specs = [vmem]
    if wave == 0:
        out_shape = (out_shape, jax.ShapeDtypeStruct((2 * IMAGES, CELLS, CELLS), bf16))
        out_specs = (vmem, vmem)
        image_specs = [pl.BlockSpec(memory_space=pltpu.HBM)] * 2
    return pl.pallas_call(
        functools.partial(pair_kernel, wave, names),
        out_shape=out_shape,
        in_specs=[smem] + [hbm] * len(names) + [vmem] * len(earlier) + image_specs + [vmem, vmem],
        out_specs=out_specs,
        scratch_shapes=[
            pltpu.VMEM((held, CELLS, CELLS), bf16),
            pltpu.VMEM((held, 16, CELLS), bf16),
            pltpu.VMEM((held, CAND), jnp.int32),
            pltpu.VMEM((4, held, CAND), jnp.int32),
            pltpu.VMEM((4 * held + 8, CELLS), f32),
            pltpu.VMEM((NODES, CAND), f32),
            pltpu.SMEM((held, CAND), jnp.int32),
            pltpu.SMEM((4 * held + UNROLL,), jnp.int32),
            pltpu.SemaphoreType.DMA((5,)),
        ],
        compiler_params=pltpu.CompilerParams(vmem_limit_bytes=12 * 2**20),
        cost_estimate=pl.CostEstimate(
            flops=3 * held * 6 * CELLS**3, bytes_accessed=16 * 2**20, transcendentals=0
        ),
    )(place, *[parts[piece][which] for piece, which in names], *earlier, *images, conv_q, conv_d)


def finish_kernel(parts_ref, scores_ref, top_ref):
    row = jnp.sum(parts_ref[...], axis=0, keepdims=True)
    scores_ref[...] = row
    across = jnp.broadcast_to(row, (CAND, CAND))
    down = across.T
    at_row = lax.broadcasted_iota(jnp.int32, (CAND, CAND), 0)
    at_col = lax.broadcasted_iota(jnp.int32, (CAND, CAND), 1)
    ahead = (across > down) | ((across == down) & (at_col < at_row))
    rank = jnp.sum(ahead.astype(f32), axis=1, keepdims=True)
    placed = jnp.where(rank == at_col.astype(f32), down, 0.0)
    top_ref[...] = jnp.sum(placed, axis=0, keepdims=True)[:, :TOPK]


def finish(parts):
    return pl.pallas_call(
        finish_kernel,
        out_shape=(
            jax.ShapeDtypeStruct((1, CAND), f32),
            jax.ShapeDtypeStruct((1, TOPK), f32),
        ),
    )(parts)


def place_table():
    me = lax.axis_index("c")
    x, y, z = [lax.axis_index(axis) for axis in NODE]
    base = (x * 4 + y) * 8 + z
    near = jnp.where(me == 0, 1, 3)
    far = 4 - near
    combos = jnp.array([combo for wave in WAVES for combo in wave], jnp.int32)
    index = (combos[:, None] * GROUP + jnp.arange(GROUP, dtype=jnp.int32)).reshape(-1)
    bit = [lax.shift_right_logical(index, k) & 1 for k in range(6)]
    z = z ^ (bit[0] * near) ^ (bit[4] * far)
    x = x ^ (bit[1] * near) ^ (bit[5] * far)
    y = y ^ (bit[2] * far) ^ (bit[3] * near)
    shards = jnp.stack([base + 4 * me, base + 4 * (1 - me)])
    return jnp.concatenate([shards, (x * 4 + y) * 4 + z]).astype(jnp.int32)


def body(query_maps, database, shortlist, kernel_query, kernel_db):
    held = pack(query_maps, shortlist)
    for count, step in enumerate(WHOLE):
        came = move(held, step)
        if count == 2:
            own, conv_q, conv_d = prepare_images(database, kernel_query, kernel_db)
            came, own = lax.optimization_barrier((came, own))
        held = jnp.concatenate([held, came], axis=0)
        if count == 1:
            database, held = lax.optimization_barrier((database, held))
    other = lax.ppermute(own, "c", [(0, 1), (1, 0)])
    place = place_table()
    pieces = split(held)
    second = [move(p, o[1]) for p, o in zip(pieces, orders())]
    third = [move(p, o[2]) for p, o in zip(pieces, orders())]
    first_scores, images = pair_scores(
        0, place, [[p] for p in pieces], (), (own, other), conv_q, conv_d
    )
    *second, first_scores = lax.optimization_barrier((*second, first_scores))
    fourth = [move(p, o[2]) for p, o in zip(second, orders())]
    parts = [list(part) for part in zip(pieces, second, third, fourth)]
    second_scores = pair_scores(1, place, parts, (), (images,), conv_q, conv_d)
    earlier = (first_scores, second_scores)
    scores = pair_scores(2, place, parts, earlier, (images,), conv_q, conv_d)
    scores = lax.all_to_all(scores, NODE, split_axis=0, concat_axis=0, tiled=True)
    return finish(scores)


def solution(mesh):
    fine = Mesh(mesh.devices.reshape(4, 4, 2, 4), MAIN)
    in_specs = (P(MAIN, None, None), P(MAIN, None, None), P(MAIN, None), P(), P())
    out_specs = (P(MAIN, None), P(MAIN, None))
    return jax.shard_map(body, mesh=fine, in_specs=in_specs, out_specs=out_specs, check_vma=False)
```

```python
import functools

import jax
import jax.numpy as jnp
from jax import lax
from jax.experimental import pallas as pl
from jax.experimental.pallas import tpu as pltpu
from jax.sharding import Mesh, PartitionSpec as P

GRID = 16
CELLS = GRID * GRID
TOPK = 100
CAND = 128
IMAGES = 32
NODES = 64
CUTS = (0, 80, 176, CELLS)
LARGE = 16
SMALL = 8

epsilon = 1e-06
score_scale = 8.0
f32 = jnp.float32
bf16 = jnp.bfloat16

MAIN = ("x", "y", "c", "z")
NODE = ("x", "y", "z")
OPENING = (("z", True), ("x", True), ("zx", True))
LATE = (("y", True), ("z", False), ("x", False))
GROUP = 8
BLOCK = 4
WAVES = ((0,), (1, 2, 4), (3, 5, 6, 7))


def exchange_pairs(axes, near):
    pairs = []
    for x in range(4):
        for y in range(4):
            for c in range(2):
                for z in range(4):
                    at = {"x": x, "y": y, "z": z}
                    to = dict(at)
                    for axis in axes:
                        to[axis] = at[axis] ^ (1 if (c == 0) == near else 3)
                    pairs.append(
                        (((x * 4 + y) * 2 + c) * 4 + z, ((to["x"] * 4 + to["y"]) * 2 + c) * 4 + to["z"])
                    )
    return pairs


PAIRS = {(axes, near): exchange_pairs(axes, near) for axes in ("x", "y", "z", "zx") for near in (True, False)}


def unit(values):
    squares = jnp.sum(values * values, axis=0, keepdims=True)
    return values * lax.rsqrt(squares + epsilon)


def pack_kernel(query_ref, ids_ref, out_ref):
    out_ref[0, 16:, :] = unit(query_ref[0].astype(f32)).T.astype(bf16)
    ids = ids_ref[...]
    high = lax.shift_right_logical(ids, 6).astype(f32)
    low = (ids & 63).astype(f32)
    row = jnp.concatenate([high, low], axis=1)
    first = lax.broadcasted_iota(jnp.int32, (16, 2 * CAND), 0) == 0
    out_ref[0, :16, :] = jnp.where(first, jnp.broadcast_to(row, first.shape), 0.0).astype(bf16)


def pack(query_maps, shortlist):
    return pl.pallas_call(
        pack_kernel,
        out_shape=jax.ShapeDtypeStruct((1, CELLS + 16, CELLS), bf16),
    )(query_maps, shortlist)


def images_kernel(tap_q_ref, tap_d_ref, maps_hbm, unit_ref, conv_q_ref, conv_d_ref, maps_v, sems):
    copies = []
    for block in range(IMAGES // BLOCK):
        here = pl.ds(block * BLOCK, BLOCK)
        copies.append(pltpu.make_async_copy(maps_hbm.at[here], maps_v.at[here], sems.at[block]))
    for copy in copies:
        copy.start()
    near = lax.broadcasted_iota(jnp.int32, (CELLS, CELLS), 0)
    far = lax.broadcasted_iota(jnp.int32, (CELLS, CELLS), 1)
    for tap_ref, out_ref, result, source in (
        (tap_q_ref, conv_q_ref, near, far),
        (tap_d_ref, conv_d_ref, far, near),
    ):
        down = lax.shift_right_logical(source, 4) - lax.shift_right_logical(result, 4)
        right = (source & (GRID - 1)) - (result & (GRID - 1))
        matrix = jnp.zeros((CELLS, CELLS), f32)
        taps = tap_ref[...].astype(f32)
        for i in range(3):
            for j in range(3):
                hit = (down == i - 1) & (right == j - 1)
                matrix = jnp.where(hit, taps[i : i + 1, j : j + 1], matrix)
        out_ref[...] = matrix.astype(bf16)
    for block, copy in enumerate(copies):
        copy.wait()
        for image in range(block * BLOCK, (block + 1) * BLOCK):
            unit_ref[image] = unit(maps_v[image].astype(f32)).astype(bf16)


def prepare_images(database, tap_q, tap_d):
    vmem = pl.BlockSpec(memory_space=pltpu.VMEM)
    square_shape = jax.ShapeDtypeStruct((CELLS, CELLS), bf16)
    return pl.pallas_call(
        images_kernel,
        in_specs=[vmem, vmem, pl.BlockSpec(memory_space=pl.ANY)],
        out_specs=(vmem, vmem, vmem),
        out_shape=(jax.ShapeDtypeStruct(database.shape, bf16), square_shape, square_shape),
        scratch_shapes=[
            pltpu.VMEM(database.shape, bf16),
            pltpu.SemaphoreType.DMA((IMAGES // BLOCK,)),
        ],
        compiler_params=pltpu.CompilerParams(vmem_limit_bytes=12 * 2**20),
        cost_estimate=pl.CostEstimate(flops=2**24, bytes_accessed=20 * 2**20, transcendentals=0),
    )(tap_q, tap_d, database)


def move(array, step):
    return lax.ppermute(array, MAIN, PAIRS[step])


def orders():
    return [(LATE[piece % 3], LATE[(piece + 1) % 3], LATE[(piece + 2) % 3]) for piece in (0, 2, 1)]


def split(held, own):
    pieces = []
    for piece in range(3):
        first = CUTS[piece] + (16 if piece else 0)
        pieces.append(held[:, first : CUTS[piece + 1] + 16])
    came = [move(p, o[0]) for p, o in zip(pieces, orders())]
    *came, own = lax.optimization_barrier((*came, own))
    return [jnp.concatenate(pair, axis=0) for pair in zip(pieces, came)], own


def sources(combo):
    bits = (combo & 1, combo >> 1 & 1, combo >> 2)
    for turn in (0, 2, 1):
        yield bits[(turn + 1) % 3] + 2 * bits[(turn + 2) % 3], bits[turn]


def pair_kernel(wave, names, place_ref, *refs):
    held = len(WAVES[wave]) * GROUP
    spare = 4 * held
    refs, scratch = refs[:-9], refs[-9:]
    query_v, ids_v, table_v, column_v, peak_v, total_v, table_s, pair_s, sems = scratch
    parts, refs = dict(zip(names, refs)), refs[len(names) :]
    earlier = ()
    if wave == 2:
        earlier, refs = refs[:2], refs[2:]
    if wave == 0:
        own_hbm, other_hbm, conv_q_ref, conv_d_ref, out_ref, image_v = refs[:6]
        image_copies = [
            pltpu.make_async_copy(own_hbm, image_v.at[pl.ds(0, IMAGES)], sems.at[2]),
            pltpu.make_async_copy(other_hbm, image_v.at[pl.ds(IMAGES, IMAGES)], sems.at[3]),
        ]
    else:
        image_v, conv_q_ref, conv_d_ref, out_ref = refs[:4]
        image_copies = []
    id_copies, copies = [], []
    for local, combo in enumerate(WAVES[wave]):
        here = pl.ds(GROUP * local, GROUP)
        for piece, (which, half) in enumerate(sources(combo)):
            source = parts[piece, which]
            blocks = pl.ds(GROUP * half, GROUP)
            size = CUTS[piece + 1] - CUTS[piece]
            skip = 0 if piece else 16
            copies.append(
                pltpu.make_async_copy(
                    source.at[blocks, pl.ds(skip, size), :],
                    query_v.at[here, pl.ds(CUTS[piece], size), :],
                    sems.at[1],
                )
            )
            if piece == 0:
                id_copies.append(
                    pltpu.make_async_copy(
                        source.at[blocks, pl.ds(0, 16), :], ids_v.at[here], sems.at[0]
                    )
                )
    for copy in id_copies + image_copies + copies:
        copy.start()
    pltpu.make_async_copy(ids_v, ids_v, sems.at[0]).wait()
    packed = jnp.sum(ids_v[...].astype(f32), axis=1)
    ids = packed[:, :CAND].astype(jnp.int32) * 64 + packed[:, CAND:].astype(jnp.int32)
    lane = lax.broadcasted_iota(jnp.int32, (held, CAND), 1)
    shard = lax.shift_right_logical(ids, 5)
    slot = ids & (IMAGES - 1)
    table = jnp.full((held, CAND), -1, jnp.int32)
    for side in range(2):
        mine = shard == place_ref[side]
        first = jnp.min(jnp.where(mine, lane, CAND), axis=1, keepdims=True)
        last = jnp.max(jnp.where(mine, lane, -1), axis=1, keepdims=True)
        last = jnp.where(last > first, last, -1)
        for which, column in ((2 * side, first), (2 * side + 1, last)):
            at = lane == column
            image = jnp.max(jnp.where(at, slot, -1), axis=1, keepdims=True)
            image = jnp.where(image >= 0, image + side * IMAGES, -1)
            table = jnp.where(lane == which, image, table)
            column_v[which] = jnp.broadcast_to(column, (held, CAND))
    table_v[...] = table
    move = pltpu.make_async_copy(table_v, table_s, sems.at[4])
    move.start()
    move.wait()

    def fill(query, count):
        for which in range(4):
            image = table_s[query, which]
            pair_s[count] = query * 65536 + (which * held + query) * 64 + jnp.maximum(image, 0)
            count = count + (image >= 0).astype(jnp.int32)
        return count

    count = lax.fori_loop(0, held, fill, jnp.int32(0))
    for extra in range(LARGE):
        pair_s[count + extra] = spare * 64
    for copy in image_copies:
        copy.wait()
    pltpu.make_async_copy(query_v, query_v, sems.at[1]).wait()

    def group(size, base, step, carry):
        found = []
        for part in range(size):
            code = pair_s[base + step * size + part]
            node = lax.shift_right_logical(code, 16)
            image = code & 63
            correlation = jnp.dot(query_v[node], image_v[image], preferred_element_type=f32)
            rectified = jnp.maximum(correlation, 0.0).astype(bf16)
            found.append((lax.shift_right_logical(code, 6) & 1023, rectified))
        for row, rectified in found:
            filtered = jnp.dot(conv_q_ref[...], rectified, preferred_element_type=f32)
            filtered = filtered + jnp.dot(rectified, conv_d_ref[...], preferred_element_type=f32)
            peak_v[pl.ds(row, 1), :] = jnp.max(filtered, axis=0, keepdims=True)
        return carry

    large = (count + LARGE - SMALL - 1) // LARGE
    rest = jnp.maximum(count - large * LARGE, 0)
    lax.fori_loop(0, large, functools.partial(group, LARGE, 0), 0)
    lax.fori_loop(0, (rest + SMALL - 1) // SMALL, functools.partial(group, SMALL, large * LARGE), 0)
    total = jnp.zeros((held, CAND), f32)
    for which in range(4):
        peaks = peak_v[pl.ds(which * held, held), :]
        score = jnp.sum(peaks, axis=1, keepdims=True) * (score_scale / CELLS)
        total = jnp.where(lane == column_v[which], score, total)
    if wave < 2:
        out_ref[...] = total
        return
    done = 0
    for ref in earlier:
        total_v[pl.ds(done, ref.shape[0]), :] = ref[...]
        done += ref.shape[0]
    total_v[pl.ds(done, held), :] = total

    def settle(query, carry):
        out_ref[pl.ds(place_ref[2 + query], 1), :] = total_v[pl.ds(query, 1), :]
        return carry

    lax.fori_loop(0, NODES, settle, 0, unroll=8)


def pair_scores(wave, place, parts, earlier, images, conv_q, conv_d):
    smem = pl.BlockSpec(memory_space=pltpu.SMEM)
    vmem = pl.BlockSpec(memory_space=pltpu.VMEM)
    hbm = pl.BlockSpec(memory_space=pl.ANY)
    held = len(WAVES[wave]) * GROUP
    names = sorted(
        {(piece, which) for combo in WAVES[wave] for piece, (which, _) in enumerate(sources(combo))}
    )
    out_shape = jax.ShapeDtypeStruct((NODES if wave == 2 else held, CAND), f32)
    out_specs = vmem
    image_specs = [vmem]
    if wave == 0:
        out_shape = (out_shape, jax.ShapeDtypeStruct((2 * IMAGES, CELLS, CELLS), bf16))
        out_specs = (vmem, vmem)
        image_specs = [pl.BlockSpec(memory_space=pltpu.HBM)] * 2
    return pl.pallas_call(
        functools.partial(pair_kernel, wave, names),
        out_shape=out_shape,
        in_specs=[smem] + [hbm] * len(names) + [vmem] * len(earlier) + image_specs + [vmem, vmem],
        out_specs=out_specs,
        scratch_shapes=[
            pltpu.VMEM((held, CELLS, CELLS), bf16),
            pltpu.VMEM((held, 16, CELLS), bf16),
            pltpu.VMEM((held, CAND), jnp.int32),
            pltpu.VMEM((4, held, CAND), jnp.int32),
            pltpu.VMEM((4 * held + 8, CELLS), f32),
            pltpu.VMEM((NODES, CAND), f32),
            pltpu.SMEM((held, CAND), jnp.int32),
            pltpu.SMEM((4 * held + LARGE,), jnp.int32),
            pltpu.SemaphoreType.DMA((5,)),
        ],
        compiler_params=pltpu.CompilerParams(vmem_limit_bytes=12 * 2**20),
        cost_estimate=pl.CostEstimate(
            flops=3 * held * 6 * CELLS**3, bytes_accessed=16 * 2**20, transcendentals=0
        ),
    )(place, *[parts[piece][which] for piece, which in names], *earlier, *images, conv_q, conv_d)


def finish_kernel(parts_ref, scores_ref, top_ref):
    row = jnp.sum(parts_ref[...], axis=0, keepdims=True)
    scores_ref[...] = row
    across = jnp.broadcast_to(row, (CAND, CAND))
    down = across.T
    at_row = lax.broadcasted_iota(jnp.int32, (CAND, CAND), 0)
    at_col = lax.broadcasted_iota(jnp.int32, (CAND, CAND), 1)
    ahead = (across > down) | ((across == down) & (at_col < at_row))
    rank = jnp.sum(ahead.astype(f32), axis=1, keepdims=True)
    placed = jnp.where(rank == at_col.astype(f32), down, 0.0)
    top_ref[...] = jnp.sum(placed, axis=0, keepdims=True)[:, :TOPK]


def finish(parts):
    return pl.pallas_call(
        finish_kernel,
        out_shape=(
            jax.ShapeDtypeStruct((1, CAND), f32),
            jax.ShapeDtypeStruct((1, TOPK), f32),
        ),
    )(parts)


def place_table():
    me = lax.axis_index("c")
    x, y, z = [lax.axis_index(axis) for axis in NODE]
    base = (x * 4 + y) * 8 + z
    near = jnp.where(me == 0, 1, 3)
    far = 4 - near
    combos = jnp.array([combo for wave in WAVES for combo in wave], jnp.int32)
    index = (combos[:, None] * GROUP + jnp.arange(GROUP, dtype=jnp.int32)).reshape(-1)
    bit = [lax.shift_right_logical(index, k) & 1 for k in range(6)]
    z = z ^ (bit[0] * near) ^ (bit[4] * far)
    x = x ^ (bit[1] * near) ^ (bit[5] * far)
    y = y ^ (bit[2] * far) ^ (bit[3] * near)
    shards = jnp.stack([base + 4 * me, base + 4 * (1 - me)])
    return jnp.concatenate([shards, (x * 4 + y) * 4 + z]).astype(jnp.int32)


def body(query_maps, database, shortlist, kernel_query, kernel_db):
    held = pack(query_maps, shortlist)
    held = jnp.concatenate([held] + [move(held, step) for step in OPENING], axis=0)
    database, held = lax.optimization_barrier((database, held))
    came = move(held, ("y", False))
    own, conv_q, conv_d = prepare_images(database, kernel_query, kernel_db)
    came, own = lax.optimization_barrier((came, own))
    held = jnp.concatenate([held, came], axis=0)
    place = place_table()
    pieces, own = split(held, own)
    other = lax.ppermute(own, "c", [(0, 1), (1, 0)])
    second = [move(p, o[1]) for p, o in zip(pieces, orders())]
    third = [move(p, o[2]) for p, o in zip(pieces, orders())]
    first_scores, images = pair_scores(
        0, place, [[p] for p in pieces], (), (own, other), conv_q, conv_d
    )
    *second, first_scores = lax.optimization_barrier((*second, first_scores))
    fourth = [move(p, o[2]) for p, o in zip(second, orders())]
    parts = [list(part) for part in zip(pieces, second, third, fourth)]
    second_scores = pair_scores(1, place, parts, (), (images,), conv_q, conv_d)
    earlier = (first_scores, second_scores)
    scores = pair_scores(2, place, parts, earlier, (images,), conv_q, conv_d)
    scores = lax.all_to_all(scores, NODE, split_axis=0, concat_axis=0, tiled=True)
    return finish(scores)


def solution(mesh):
    fine = Mesh(mesh.devices.reshape(4, 4, 2, 4), MAIN)
    in_specs = (P(MAIN, None, None), P(MAIN, None, None), P(MAIN, None), P(), P())
    out_specs = (P(MAIN, None), P(MAIN, None))
    return jax.shard_map(body, mesh=fine, in_specs=in_specs, out_specs=out_specs, check_vma=False)
```

```python
import functools

import jax
import jax.numpy as jnp
from jax import lax
from jax.experimental import pallas as pl
from jax.experimental.pallas import tpu as pltpu
from jax.sharding import Mesh, PartitionSpec as P

GRID = 16
CELLS = GRID * GRID
TOPK = 100
CAND = 128
IMAGES = 32
NODES = 64
CUTS = (0, 80, 176, CELLS)
LARGE = 16
SMALL = 8

epsilon = 1e-06
score_scale = 8.0
f32 = jnp.float32
bf16 = jnp.bfloat16

MAIN = ("x", "y", "c", "z")
NODE = ("x", "y", "z")
FIRST = (("z", True), ("x", True), ("y", False))
OPENING = tuple(tuple(FIRST[k] for k in range(3) if code >> k & 1) for code in range(1, 8))
LATE = ((("y", True),), (("z", False),), (("x", False),))
STEPS = OPENING + LATE
GROUP = 8
BLOCK = 4
WAVES = ((0,), (1, 2, 4), (3, 5, 6, 7))


def exchange_pairs(turns):
    pairs = []
    for x in range(4):
        for y in range(4):
            for c in range(2):
                for z in range(4):
                    at = {"x": x, "y": y, "z": z}
                    to = dict(at)
                    for axis, near in turns:
                        to[axis] = at[axis] ^ (1 if (c == 0) == near else 3)
                    pairs.append(
                        (((x * 4 + y) * 2 + c) * 4 + z, ((to["x"] * 4 + to["y"]) * 2 + c) * 4 + to["z"])
                    )
    return pairs


PAIRS = {step: exchange_pairs(step) for step in STEPS}


def unit(values):
    squares = jnp.sum(values * values, axis=0, keepdims=True)
    return values * lax.rsqrt(squares + epsilon)


def pack_kernel(query_ref, ids_ref, out_ref):
    out_ref[0, 16:, :] = unit(query_ref[0].astype(f32)).T.astype(bf16)
    ids = ids_ref[...]
    high = lax.shift_right_logical(ids, 6).astype(f32)
    low = (ids & 63).astype(f32)
    row = jnp.concatenate([high, low], axis=1)
    first = lax.broadcasted_iota(jnp.int32, (16, 2 * CAND), 0) == 0
    out_ref[0, :16, :] = jnp.where(first, jnp.broadcast_to(row, first.shape), 0.0).astype(bf16)


def pack(query_maps, shortlist):
    return pl.pallas_call(
        pack_kernel,
        out_shape=jax.ShapeDtypeStruct((1, CELLS + 16, CELLS), bf16),
    )(query_maps, shortlist)


def images_kernel(tap_q_ref, tap_d_ref, maps_hbm, unit_ref, conv_q_ref, conv_d_ref, maps_v, sems):
    copies = []
    for block in range(IMAGES // BLOCK):
        here = pl.ds(block * BLOCK, BLOCK)
        copies.append(pltpu.make_async_copy(maps_hbm.at[here], maps_v.at[here], sems.at[block]))
    for copy in copies:
        copy.start()
    near = lax.broadcasted_iota(jnp.int32, (CELLS, CELLS), 0)
    far = lax.broadcasted_iota(jnp.int32, (CELLS, CELLS), 1)
    for tap_ref, out_ref, result, source in (
        (tap_q_ref, conv_q_ref, near, far),
        (tap_d_ref, conv_d_ref, far, near),
    ):
        down = lax.shift_right_logical(source, 4) - lax.shift_right_logical(result, 4)
        right = (source & (GRID - 1)) - (result & (GRID - 1))
        matrix = jnp.zeros((CELLS, CELLS), f32)
        taps = tap_ref[...].astype(f32)
        for i in range(3):
            for j in range(3):
                hit = (down == i - 1) & (right == j - 1)
                matrix = jnp.where(hit, taps[i : i + 1, j : j + 1], matrix)
        out_ref[...] = matrix.astype(bf16)
    for block, copy in enumerate(copies):
        copy.wait()
        for image in range(block * BLOCK, (block + 1) * BLOCK):
            unit_ref[image] = unit(maps_v[image].astype(f32)).astype(bf16)


def prepare_images(database, tap_q, tap_d):
    vmem = pl.BlockSpec(memory_space=pltpu.VMEM)
    square_shape = jax.ShapeDtypeStruct((CELLS, CELLS), bf16)
    return pl.pallas_call(
        images_kernel,
        in_specs=[vmem, vmem, pl.BlockSpec(memory_space=pl.ANY)],
        out_specs=(vmem, vmem, vmem),
        out_shape=(jax.ShapeDtypeStruct(database.shape, bf16), square_shape, square_shape),
        scratch_shapes=[
            pltpu.VMEM(database.shape, bf16),
            pltpu.SemaphoreType.DMA((IMAGES // BLOCK,)),
        ],
        compiler_params=pltpu.CompilerParams(vmem_limit_bytes=12 * 2**20),
        cost_estimate=pl.CostEstimate(flops=2**24, bytes_accessed=20 * 2**20, transcendentals=0),
    )(tap_q, tap_d, database)


def move(array, step):
    return lax.ppermute(array, MAIN, PAIRS[step])


def orders():
    return [(LATE[piece % 3], LATE[(piece + 1) % 3], LATE[(piece + 2) % 3]) for piece in (0, 2, 1)]


def split(held, own):
    pieces = []
    for piece in range(3):
        first = CUTS[piece] + (16 if piece else 0)
        pieces.append(held[:, first : CUTS[piece + 1] + 16])
    came = [move(p, o[0]) for p, o in zip(pieces, orders())]
    *came, own = lax.optimization_barrier((*came, own))
    return [jnp.concatenate(pair, axis=0) for pair in zip(pieces, came)], own


def sources(combo):
    bits = (combo & 1, combo >> 1 & 1, combo >> 2)
    for turn in (0, 2, 1):
        yield bits[(turn + 1) % 3] + 2 * bits[(turn + 2) % 3], bits[turn]


def pair_kernel(wave, names, place_ref, *refs):
    held = len(WAVES[wave]) * GROUP
    spare = 4 * held
    refs, scratch = refs[:-9], refs[-9:]
    query_v, ids_v, table_v, column_v, peak_v, total_v, table_s, pair_s, sems = scratch
    parts, refs = dict(zip(names, refs)), refs[len(names) :]
    earlier = ()
    if wave == 2:
        earlier, refs = refs[:2], refs[2:]
    if wave == 0:
        own_hbm, other_hbm, conv_q_ref, conv_d_ref, out_ref, image_v = refs[:6]
        image_copies = [
            pltpu.make_async_copy(own_hbm, image_v.at[pl.ds(0, IMAGES)], sems.at[2]),
            pltpu.make_async_copy(other_hbm, image_v.at[pl.ds(IMAGES, IMAGES)], sems.at[3]),
        ]
    else:
        image_v, conv_q_ref, conv_d_ref, out_ref = refs[:4]
        image_copies = []
    id_copies, copies = [], []
    for local, combo in enumerate(WAVES[wave]):
        here = pl.ds(GROUP * local, GROUP)
        for piece, (which, half) in enumerate(sources(combo)):
            source = parts[piece, which]
            blocks = pl.ds(GROUP * half, GROUP)
            size = CUTS[piece + 1] - CUTS[piece]
            skip = 0 if piece else 16
            copies.append(
                pltpu.make_async_copy(
                    source.at[blocks, pl.ds(skip, size), :],
                    query_v.at[here, pl.ds(CUTS[piece], size), :],
                    sems.at[1],
                )
            )
            if piece == 0:
                id_copies.append(
                    pltpu.make_async_copy(
                        source.at[blocks, pl.ds(0, 16), :], ids_v.at[here], sems.at[0]
                    )
                )
    for copy in id_copies + image_copies + copies:
        copy.start()
    pltpu.make_async_copy(ids_v, ids_v, sems.at[0]).wait()
    packed = jnp.sum(ids_v[...].astype(f32), axis=1)
    ids = packed[:, :CAND].astype(jnp.int32) * 64 + packed[:, CAND:].astype(jnp.int32)
    lane = lax.broadcasted_iota(jnp.int32, (held, CAND), 1)
    shard = lax.shift_right_logical(ids, 5)
    slot = ids & (IMAGES - 1)
    table = jnp.full((held, CAND), -1, jnp.int32)
    for side in range(2):
        mine = shard == place_ref[side]
        first = jnp.min(jnp.where(mine, lane, CAND), axis=1, keepdims=True)
        last = jnp.max(jnp.where(mine, lane, -1), axis=1, keepdims=True)
        last = jnp.where(last > first, last, -1)
        for which, column in ((2 * side, first), (2 * side + 1, last)):
            at = lane == column
            image = jnp.max(jnp.where(at, slot, -1), axis=1, keepdims=True)
            image = jnp.where(image >= 0, image + side * IMAGES, -1)
            table = jnp.where(lane == which, image, table)
            column_v[which] = jnp.broadcast_to(column, (held, CAND))
    table_v[...] = table
    move = pltpu.make_async_copy(table_v, table_s, sems.at[4])
    move.start()
    move.wait()

    def fill(query, count):
        for which in range(4):
            image = table_s[query, which]
            pair_s[count] = query * 65536 + (which * held + query) * 64 + jnp.maximum(image, 0)
            count = count + (image >= 0).astype(jnp.int32)
        return count

    count = lax.fori_loop(0, held, fill, jnp.int32(0))
    for extra in range(LARGE):
        pair_s[count + extra] = spare * 64
    for copy in image_copies:
        copy.wait()
    pltpu.make_async_copy(query_v, query_v, sems.at[1]).wait()

    def group(size, base, step, carry):
        found = []
        for part in range(size):
            code = pair_s[base + step * size + part]
            node = lax.shift_right_logical(code, 16)
            image = code & 63
            correlation = jnp.dot(query_v[node], image_v[image], preferred_element_type=f32)
            rectified = jnp.maximum(correlation, 0.0).astype(bf16)
            found.append((lax.shift_right_logical(code, 6) & 1023, rectified))
        for row, rectified in found:
            filtered = jnp.dot(conv_q_ref[...], rectified, preferred_element_type=f32)
            filtered = filtered + jnp.dot(rectified, conv_d_ref[...], preferred_element_type=f32)
            peak_v[pl.ds(row, 1), :] = jnp.max(filtered, axis=0, keepdims=True)
        return carry

    large = (count + LARGE - SMALL - 1) // LARGE
    rest = jnp.maximum(count - large * LARGE, 0)
    lax.fori_loop(0, large, functools.partial(group, LARGE, 0), 0)
    lax.fori_loop(0, (rest + SMALL - 1) // SMALL, functools.partial(group, SMALL, large * LARGE), 0)
    total = jnp.zeros((held, CAND), f32)
    for which in range(4):
        peaks = peak_v[pl.ds(which * held, held), :]
        score = jnp.sum(peaks, axis=1, keepdims=True) * (score_scale / CELLS)
        total = jnp.where(lane == column_v[which], score, total)
    if wave < 2:
        out_ref[...] = total
        return
    done = 0
    for ref in earlier:
        total_v[pl.ds(done, ref.shape[0]), :] = ref[...]
        done += ref.shape[0]
    total_v[pl.ds(done, held), :] = total

    def settle(query, carry):
        out_ref[pl.ds(place_ref[2 + query], 1), :] = total_v[pl.ds(query, 1), :]
        return carry

    lax.fori_loop(0, NODES, settle, 0, unroll=8)


def pair_scores(wave, place, parts, earlier, images, conv_q, conv_d):
    smem = pl.BlockSpec(memory_space=pltpu.SMEM)
    vmem = pl.BlockSpec(memory_space=pltpu.VMEM)
    hbm = pl.BlockSpec(memory_space=pl.ANY)
    held = len(WAVES[wave]) * GROUP
    names = sorted(
        {(piece, which) for combo in WAVES[wave] for piece, (which, _) in enumerate(sources(combo))}
    )
    out_shape = jax.ShapeDtypeStruct((NODES if wave == 2 else held, CAND), f32)
    out_specs = vmem
    image_specs = [vmem]
    if wave == 0:
        out_shape = (out_shape, jax.ShapeDtypeStruct((2 * IMAGES, CELLS, CELLS), bf16))
        out_specs = (vmem, vmem)
        image_specs = [pl.BlockSpec(memory_space=pltpu.HBM)] * 2
    return pl.pallas_call(
        functools.partial(pair_kernel, wave, names),
        out_shape=out_shape,
        in_specs=[smem] + [hbm] * len(names) + [vmem] * len(earlier) + image_specs + [vmem, vmem],
        out_specs=out_specs,
        scratch_shapes=[
            pltpu.VMEM((held, CELLS, CELLS), bf16),
            pltpu.VMEM((held, 16, CELLS), bf16),
            pltpu.VMEM((held, CAND), jnp.int32),
            pltpu.VMEM((4, held, CAND), jnp.int32),
            pltpu.VMEM((4 * held + 8, CELLS), f32),
            pltpu.VMEM((NODES, CAND), f32),
            pltpu.SMEM((held, CAND), jnp.int32),
            pltpu.SMEM((4 * held + LARGE,), jnp.int32),
            pltpu.SemaphoreType.DMA((5,)),
        ],
        compiler_params=pltpu.CompilerParams(vmem_limit_bytes=12 * 2**20),
        cost_estimate=pl.CostEstimate(
            flops=3 * held * 6 * CELLS**3, bytes_accessed=16 * 2**20, transcendentals=0
        ),
    )(place, *[parts[piece][which] for piece, which in names], *earlier, *images, conv_q, conv_d)


def finish_kernel(parts_ref, scores_ref, top_ref):
    row = jnp.sum(parts_ref[...], axis=0, keepdims=True)
    scores_ref[...] = row
    across = jnp.broadcast_to(row, (CAND, CAND))
    down = across.T
    at_row = lax.broadcasted_iota(jnp.int32, (CAND, CAND), 0)
    at_col = lax.broadcasted_iota(jnp.int32, (CAND, CAND), 1)
    ahead = (across > down) | ((across == down) & (at_col < at_row))
    rank = jnp.sum(ahead.astype(f32), axis=1, keepdims=True)
    placed = jnp.where(rank == at_col.astype(f32), down, 0.0)
    top_ref[...] = jnp.sum(placed, axis=0, keepdims=True)[:, :TOPK]


def finish(parts):
    return pl.pallas_call(
        finish_kernel,
        out_shape=(
            jax.ShapeDtypeStruct((1, CAND), f32),
            jax.ShapeDtypeStruct((1, TOPK), f32),
        ),
    )(parts)


def place_table():
    me = lax.axis_index("c")
    x, y, z = [lax.axis_index(axis) for axis in NODE]
    base = (x * 4 + y) * 8 + z
    near = jnp.where(me == 0, 1, 3)
    far = 4 - near
    combos = jnp.array([combo for wave in WAVES for combo in wave], jnp.int32)
    index = (combos[:, None] * GROUP + jnp.arange(GROUP, dtype=jnp.int32)).reshape(-1)
    bit = [lax.shift_right_logical(index, k) & 1 for k in range(6)]
    z = z ^ (bit[0] * near) ^ (bit[4] * far)
    x = x ^ (bit[1] * near) ^ (bit[5] * far)
    y = y ^ (bit[2] * far) ^ (bit[3] * near)
    shards = jnp.stack([base + 4 * me, base + 4 * (1 - me)])
    return jnp.concatenate([shards, (x * 4 + y) * 4 + z]).astype(jnp.int32)


def body(query_maps, database, shortlist, kernel_query, kernel_db):
    held = pack(query_maps, shortlist)
    held = jnp.concatenate([held] + [move(held, step) for step in OPENING], axis=0)
    database, held = lax.optimization_barrier((database, held))
    own, conv_q, conv_d = prepare_images(database, kernel_query, kernel_db)
    place = place_table()
    pieces, own = split(held, own)
    other = lax.ppermute(own, "c", [(0, 1), (1, 0)])
    second = [move(p, o[1]) for p, o in zip(pieces, orders())]
    third = [move(p, o[2]) for p, o in zip(pieces, orders())]
    first_scores, images = pair_scores(
        0, place, [[p] for p in pieces], (), (own, other), conv_q, conv_d
    )
    *second, first_scores = lax.optimization_barrier((*second, first_scores))
    fourth = [move(p, o[2]) for p, o in zip(second, orders())]
    parts = [list(part) for part in zip(pieces, second, third, fourth)]
    second_scores = pair_scores(1, place, parts, (), (images,), conv_q, conv_d)
    earlier = (first_scores, second_scores)
    scores = pair_scores(2, place, parts, earlier, (images,), conv_q, conv_d)
    scores = lax.all_to_all(scores, NODE, split_axis=0, concat_axis=0, tiled=True)
    return finish(scores)


def solution(mesh):
    fine = Mesh(mesh.devices.reshape(4, 4, 2, 4), MAIN)
    in_specs = (P(MAIN, None, None), P(MAIN, None, None), P(MAIN, None), P(), P())
    out_specs = (P(MAIN, None), P(MAIN, None))
    return jax.shard_map(body, mesh=fine, in_specs=in_specs, out_specs=out_specs, check_vma=False)
```

```python
import functools

import jax
import jax.numpy as jnp
from jax import lax
from jax.experimental import pallas as pl
from jax.experimental.pallas import tpu as pltpu
from jax.sharding import Mesh, PartitionSpec as P

GRID = 16
CELLS = GRID * GRID
TOPK = 100
CAND = 128
IMAGES = 32
NODES = 64
CUTS = (0, 80, 176, CELLS)
LARGE = 24
SMALL = 8

epsilon = 1e-06
score_scale = 8.0
f32 = jnp.float32
bf16 = jnp.bfloat16

MAIN = ("x", "y", "c", "z")
NODE = ("x", "y", "z")
FIRST = (("z", True), ("x", True), ("y", False))
OPENING = tuple(tuple(FIRST[k] for k in range(3) if code >> k & 1) for code in range(1, 8))
LATE = ((("y", True),), (("z", False),), (("x", False),))
STEPS = OPENING + LATE
GROUP = 8
BLOCK = 4
WAVES = ((0,), (1, 2, 4), (3, 5, 6, 7))


def exchange_pairs(turns):
    pairs = []
    for x in range(4):
        for y in range(4):
            for c in range(2):
                for z in range(4):
                    at = {"x": x, "y": y, "z": z}
                    to = dict(at)
                    for axis, near in turns:
                        to[axis] = at[axis] ^ (1 if (c == 0) == near else 3)
                    pairs.append(
                        (((x * 4 + y) * 2 + c) * 4 + z, ((to["x"] * 4 + to["y"]) * 2 + c) * 4 + to["z"])
                    )
    return pairs


PAIRS = {step: exchange_pairs(step) for step in STEPS}


def unit(values):
    squares = jnp.sum(values * values, axis=0, keepdims=True)
    return values * lax.rsqrt(squares + epsilon)


def pack_kernel(query_ref, ids_ref, out_ref):
    out_ref[0, 16:, :] = unit(query_ref[0].astype(f32)).T.astype(bf16)
    ids = ids_ref[...]
    high = lax.shift_right_logical(ids, 6).astype(f32)
    low = (ids & 63).astype(f32)
    row = jnp.concatenate([high, low], axis=1)
    first = lax.broadcasted_iota(jnp.int32, (16, 2 * CAND), 0) == 0
    out_ref[0, :16, :] = jnp.where(first, jnp.broadcast_to(row, first.shape), 0.0).astype(bf16)


def pack(query_maps, shortlist):
    return pl.pallas_call(
        pack_kernel,
        out_shape=jax.ShapeDtypeStruct((1, CELLS + 16, CELLS), bf16),
    )(query_maps, shortlist)


def images_kernel(tap_q_ref, tap_d_ref, maps_hbm, unit_ref, conv_q_ref, conv_d_ref, maps_v, sems):
    copies = []
    for block in range(IMAGES // BLOCK):
        here = pl.ds(block * BLOCK, BLOCK)
        copies.append(pltpu.make_async_copy(maps_hbm.at[here], maps_v.at[here], sems.at[block]))
    for copy in copies:
        copy.start()
    near = lax.broadcasted_iota(jnp.int32, (CELLS, CELLS), 0)
    far = lax.broadcasted_iota(jnp.int32, (CELLS, CELLS), 1)
    for tap_ref, out_ref, result, source in (
        (tap_q_ref, conv_q_ref, near, far),
        (tap_d_ref, conv_d_ref, far, near),
    ):
        down = lax.shift_right_logical(source, 4) - lax.shift_right_logical(result, 4)
        right = (source & (GRID - 1)) - (result & (GRID - 1))
        matrix = jnp.zeros((CELLS, CELLS), f32)
        taps = tap_ref[...].astype(f32)
        for i in range(3):
            for j in range(3):
                hit = (down == i - 1) & (right == j - 1)
                matrix = jnp.where(hit, taps[i : i + 1, j : j + 1], matrix)
        out_ref[...] = matrix.astype(bf16)
    for block, copy in enumerate(copies):
        copy.wait()
        for image in range(block * BLOCK, (block + 1) * BLOCK):
            unit_ref[image] = unit(maps_v[image].astype(f32)).astype(bf16)


def prepare_images(database, tap_q, tap_d):
    vmem = pl.BlockSpec(memory_space=pltpu.VMEM)
    square_shape = jax.ShapeDtypeStruct((CELLS, CELLS), bf16)
    return pl.pallas_call(
        images_kernel,
        in_specs=[vmem, vmem, pl.BlockSpec(memory_space=pl.ANY)],
        out_specs=(vmem, vmem, vmem),
        out_shape=(jax.ShapeDtypeStruct(database.shape, bf16), square_shape, square_shape),
        scratch_shapes=[
            pltpu.VMEM(database.shape, bf16),
            pltpu.SemaphoreType.DMA((IMAGES // BLOCK,)),
        ],
        compiler_params=pltpu.CompilerParams(vmem_limit_bytes=12 * 2**20),
        cost_estimate=pl.CostEstimate(flops=2**24, bytes_accessed=20 * 2**20, transcendentals=0),
    )(tap_q, tap_d, database)


def move(array, step):
    return lax.ppermute(array, MAIN, PAIRS[step])


def orders():
    return [(LATE[piece % 3], LATE[(piece + 1) % 3], LATE[(piece + 2) % 3]) for piece in (0, 2, 1)]


def split(held, own):
    pieces = []
    for piece in range(3):
        first = CUTS[piece] + (16 if piece else 0)
        pieces.append(held[:, first : CUTS[piece + 1] + 16])
    came = [move(p, o[0]) for p, o in zip(pieces, orders())]
    *came, own = lax.optimization_barrier((*came, own))
    return [jnp.concatenate(pair, axis=0) for pair in zip(pieces, came)], own


def sources(combo):
    bits = (combo & 1, combo >> 1 & 1, combo >> 2)
    for turn in (0, 2, 1):
        yield bits[(turn + 1) % 3] + 2 * bits[(turn + 2) % 3], bits[turn]


def pair_kernel(wave, names, place_ref, *refs):
    held = len(WAVES[wave]) * GROUP
    spare = 4 * held
    refs, scratch = refs[:-9], refs[-9:]
    query_v, ids_v, table_v, column_v, peak_v, total_v, table_s, pair_s, sems = scratch
    parts, refs = dict(zip(names, refs)), refs[len(names) :]
    earlier = ()
    if wave == 2:
        earlier, refs = refs[:2], refs[2:]
    if wave == 0:
        own_hbm, other_hbm, conv_q_ref, conv_d_ref, out_ref, image_v = refs[:6]
        image_copies = [
            pltpu.make_async_copy(own_hbm, image_v.at[pl.ds(0, IMAGES)], sems.at[2]),
            pltpu.make_async_copy(other_hbm, image_v.at[pl.ds(IMAGES, IMAGES)], sems.at[3]),
        ]
    else:
        image_v, conv_q_ref, conv_d_ref, out_ref = refs[:4]
        image_copies = []
    id_copies, copies = [], []
    for local, combo in enumerate(WAVES[wave]):
        here = pl.ds(GROUP * local, GROUP)
        for piece, (which, half) in enumerate(sources(combo)):
            source = parts[piece, which]
            blocks = pl.ds(GROUP * half, GROUP)
            size = CUTS[piece + 1] - CUTS[piece]
            skip = 0 if piece else 16
            copies.append(
                pltpu.make_async_copy(
                    source.at[blocks, pl.ds(skip, size), :],
                    query_v.at[here, pl.ds(CUTS[piece], size), :],
                    sems.at[1],
                )
            )
            if piece == 0:
                id_copies.append(
                    pltpu.make_async_copy(
                        source.at[blocks, pl.ds(0, 16), :], ids_v.at[here], sems.at[0]
                    )
                )
    for copy in id_copies + image_copies + copies:
        copy.start()
    pltpu.make_async_copy(ids_v, ids_v, sems.at[0]).wait()
    packed = jnp.sum(ids_v[...].astype(f32), axis=1)
    ids = packed[:, :CAND].astype(jnp.int32) * 64 + packed[:, CAND:].astype(jnp.int32)
    lane = lax.broadcasted_iota(jnp.int32, (held, CAND), 1)
    shard = lax.shift_right_logical(ids, 5)
    slot = ids & (IMAGES - 1)
    table = jnp.full((held, CAND), -1, jnp.int32)
    for side in range(2):
        mine = shard == place_ref[side]
        first = jnp.min(jnp.where(mine, lane, CAND), axis=1, keepdims=True)
        last = jnp.max(jnp.where(mine, lane, -1), axis=1, keepdims=True)
        last = jnp.where(last > first, last, -1)
        for which, column in ((2 * side, first), (2 * side + 1, last)):
            at = lane == column
            image = jnp.max(jnp.where(at, slot, -1), axis=1, keepdims=True)
            image = jnp.where(image >= 0, image + side * IMAGES, -1)
            table = jnp.where(lane == which, image, table)
            column_v[which] = jnp.broadcast_to(column, (held, CAND))
    table_v[...] = table
    move = pltpu.make_async_copy(table_v, table_s, sems.at[4])
    move.start()
    move.wait()

    def fill(query, count):
        for which in range(4):
            image = table_s[query, which]
            pair_s[count] = query * 65536 + (which * held + query) * 64 + jnp.maximum(image, 0)
            count = count + (image >= 0).astype(jnp.int32)
        return count

    count = lax.fori_loop(0, held, fill, jnp.int32(0), unroll=8)
    for extra in range(LARGE):
        pair_s[count + extra] = spare * 64
    for copy in image_copies:
        copy.wait()
    pltpu.make_async_copy(query_v, query_v, sems.at[1]).wait()

    def group(size, base, step, carry):
        found = []
        for part in range(size):
            code = pair_s[base + step * size + part]
            node = lax.shift_right_logical(code, 16)
            image = code & 63
            correlation = jnp.dot(query_v[node], image_v[image], preferred_element_type=f32)
            rectified = jnp.maximum(correlation, 0.0).astype(bf16)
            found.append((lax.shift_right_logical(code, 6) & 1023, rectified))
        for row, rectified in found:
            filtered = jnp.dot(conv_q_ref[...], rectified, preferred_element_type=f32)
            filtered = filtered + jnp.dot(rectified, conv_d_ref[...], preferred_element_type=f32)
            peak_v[pl.ds(row, 1), :] = jnp.max(filtered, axis=0, keepdims=True)
        return carry

    large = (count + LARGE - SMALL - 1) // LARGE
    rest = jnp.maximum(count - large * LARGE, 0)
    lax.fori_loop(0, large, functools.partial(group, LARGE, 0), 0)
    lax.fori_loop(0, (rest + SMALL - 1) // SMALL, functools.partial(group, SMALL, large * LARGE), 0)
    total = jnp.zeros((held, CAND), f32)
    for which in range(4):
        peaks = peak_v[pl.ds(which * held, held), :]
        score = jnp.sum(peaks, axis=1, keepdims=True) * (score_scale / CELLS)
        total = jnp.where(lane == column_v[which], score, total)
    if wave < 2:
        out_ref[...] = total
        return
    done = 0
    for ref in earlier:
        total_v[pl.ds(done, ref.shape[0]), :] = ref[...]
        done += ref.shape[0]
    total_v[pl.ds(done, held), :] = total

    def settle(query, carry):
        out_ref[pl.ds(place_ref[2 + query], 1), :] = total_v[pl.ds(query, 1), :]
        return carry

    lax.fori_loop(0, NODES, settle, 0, unroll=8)


def pair_scores(wave, place, parts, earlier, images, conv_q, conv_d):
    smem = pl.BlockSpec(memory_space=pltpu.SMEM)
    vmem = pl.BlockSpec(memory_space=pltpu.VMEM)
    hbm = pl.BlockSpec(memory_space=pl.ANY)
    held = len(WAVES[wave]) * GROUP
    names = sorted(
        {(piece, which) for combo in WAVES[wave] for piece, (which, _) in enumerate(sources(combo))}
    )
    out_shape = jax.ShapeDtypeStruct((NODES if wave == 2 else held, CAND), f32)
    out_specs = vmem
    image_specs = [vmem]
    if wave == 0:
        out_shape = (out_shape, jax.ShapeDtypeStruct((2 * IMAGES, CELLS, CELLS), bf16))
        out_specs = (vmem, vmem)
        image_specs = [pl.BlockSpec(memory_space=pltpu.HBM)] * 2
    return pl.pallas_call(
        functools.partial(pair_kernel, wave, names),
        out_shape=out_shape,
        in_specs=[smem] + [hbm] * len(names) + [vmem] * len(earlier) + image_specs + [vmem, vmem],
        out_specs=out_specs,
        scratch_shapes=[
            pltpu.VMEM((held, CELLS, CELLS), bf16),
            pltpu.VMEM((held, 16, CELLS), bf16),
            pltpu.VMEM((held, CAND), jnp.int32),
            pltpu.VMEM((4, held, CAND), jnp.int32),
            pltpu.VMEM((4 * held + 8, CELLS), f32),
            pltpu.VMEM((NODES, CAND), f32),
            pltpu.SMEM((held, CAND), jnp.int32),
            pltpu.SMEM((4 * held + LARGE,), jnp.int32),
            pltpu.SemaphoreType.DMA((5,)),
        ],
        compiler_params=pltpu.CompilerParams(vmem_limit_bytes=12 * 2**20),
        cost_estimate=pl.CostEstimate(
            flops=3 * held * 6 * CELLS**3, bytes_accessed=16 * 2**20, transcendentals=0
        ),
    )(place, *[parts[piece][which] for piece, which in names], *earlier, *images, conv_q, conv_d)


def finish_kernel(parts_ref, scores_ref, top_ref):
    row = jnp.sum(parts_ref[...], axis=0, keepdims=True)
    scores_ref[...] = row
    across = jnp.broadcast_to(row, (CAND, CAND))
    down = across.T
    at_row = lax.broadcasted_iota(jnp.int32, (CAND, CAND), 0)
    at_col = lax.broadcasted_iota(jnp.int32, (CAND, CAND), 1)
    ahead = (across > down) | ((across == down) & (at_col < at_row))
    rank = jnp.sum(ahead.astype(f32), axis=1, keepdims=True)
    placed = jnp.where(rank == at_col.astype(f32), down, 0.0)
    top_ref[...] = jnp.sum(placed, axis=0, keepdims=True)[:, :TOPK]


def finish(parts):
    return pl.pallas_call(
        finish_kernel,
        out_shape=(
            jax.ShapeDtypeStruct((1, CAND), f32),
            jax.ShapeDtypeStruct((1, TOPK), f32),
        ),
    )(parts)


def place_table():
    me = lax.axis_index("c")
    x, y, z = [lax.axis_index(axis) for axis in NODE]
    base = (x * 4 + y) * 8 + z
    near = jnp.where(me == 0, 1, 3)
    far = 4 - near
    combos = jnp.array([combo for wave in WAVES for combo in wave], jnp.int32)
    index = (combos[:, None] * GROUP + jnp.arange(GROUP, dtype=jnp.int32)).reshape(-1)
    bit = [lax.shift_right_logical(index, k) & 1 for k in range(6)]
    z = z ^ (bit[0] * near) ^ (bit[4] * far)
    x = x ^ (bit[1] * near) ^ (bit[5] * far)
    y = y ^ (bit[2] * far) ^ (bit[3] * near)
    shards = jnp.stack([base + 4 * me, base + 4 * (1 - me)])
    return jnp.concatenate([shards, (x * 4 + y) * 4 + z]).astype(jnp.int32)


def body(query_maps, database, shortlist, kernel_query, kernel_db):
    held = pack(query_maps, shortlist)
    held = jnp.concatenate([held] + [move(held, step) for step in OPENING], axis=0)
    database, held = lax.optimization_barrier((database, held))
    own, conv_q, conv_d = prepare_images(database, kernel_query, kernel_db)
    place = place_table()
    pieces, own = split(held, own)
    other = lax.ppermute(own, "c", [(0, 1), (1, 0)])
    second = [move(p, o[1]) for p, o in zip(pieces, orders())]
    third = [move(p, o[2]) for p, o in zip(pieces, orders())]
    first_scores, images = pair_scores(
        0, place, [[p] for p in pieces], (), (own, other), conv_q, conv_d
    )
    *second, first_scores = lax.optimization_barrier((*second, first_scores))
    fourth = [move(p, o[2]) for p, o in zip(second, orders())]
    parts = [list(part) for part in zip(pieces, second, third, fourth)]
    second_scores = pair_scores(1, place, parts, (), (images,), conv_q, conv_d)
    earlier = (first_scores, second_scores)
    scores = pair_scores(2, place, parts, earlier, (images,), conv_q, conv_d)
    scores = lax.all_to_all(scores, NODE, split_axis=0, concat_axis=0, tiled=True)
    return finish(scores)


def solution(mesh):
    fine = Mesh(mesh.devices.reshape(4, 4, 2, 4), MAIN)
    in_specs = (P(MAIN, None, None), P(MAIN, None, None), P(MAIN, None), P(), P())
    out_specs = (P(MAIN, None), P(MAIN, None))
    return jax.shard_map(body, mesh=fine, in_specs=in_specs, out_specs=out_specs, check_vma=False)
```

```python
import functools

import jax
import jax.numpy as jnp
from jax import lax
from jax.experimental import pallas as pl
from jax.experimental.pallas import tpu as pltpu
from jax.sharding import Mesh, PartitionSpec as P

GRID = 16
CELLS = GRID * GRID
TOPK = 100
CAND = 128
IMAGES = 32
NODES = 64
CUTS = (0, 80, 176, CELLS)
LARGE = 24
SMALL = 8

epsilon = 1e-06
score_scale = 8.0
f32 = jnp.float32
bf16 = jnp.bfloat16

MAIN = ("x", "y", "c", "z")
NODE = ("x", "y", "z")
FIRST = (("z", True), ("x", True), ("y", False))
OPENING = tuple(tuple(FIRST[k] for k in range(3) if code >> k & 1) for code in range(1, 8))
LATE = ((("y", True),), (("z", False),), (("x", False),))
STEPS = OPENING + LATE
GROUP = 8
BLOCK = 4
WAVES = ((0,), (1, 2, 4), (3, 5, 6, 7))


def exchange_pairs(turns):
    pairs = []
    for x in range(4):
        for y in range(4):
            for c in range(2):
                for z in range(4):
                    at = {"x": x, "y": y, "z": z}
                    to = dict(at)
                    for axis, near in turns:
                        to[axis] = at[axis] ^ (1 if (c == 0) == near else 3)
                    pairs.append(
                        (((x * 4 + y) * 2 + c) * 4 + z, ((to["x"] * 4 + to["y"]) * 2 + c) * 4 + to["z"])
                    )
    return pairs


PAIRS = {step: exchange_pairs(step) for step in STEPS}


def unit(values):
    squares = jnp.sum(values * values, axis=0, keepdims=True)
    return values * lax.rsqrt(squares + epsilon)


def pack_kernel(query_ref, ids_ref, out_ref):
    out_ref[0, 16:, :] = unit(query_ref[0].astype(f32)).T.astype(bf16)
    ids = ids_ref[...]
    high = lax.shift_right_logical(ids, 6).astype(f32)
    low = (ids & 63).astype(f32)
    row = jnp.concatenate([high, low], axis=1)
    first = lax.broadcasted_iota(jnp.int32, (16, 2 * CAND), 0) == 0
    out_ref[0, :16, :] = jnp.where(first, jnp.broadcast_to(row, first.shape), 0.0).astype(bf16)


def pack(query_maps, shortlist):
    return pl.pallas_call(
        pack_kernel,
        out_shape=jax.ShapeDtypeStruct((1, CELLS + 16, CELLS), bf16),
    )(query_maps, shortlist)


def images_kernel(tap_q_ref, tap_d_ref, maps_hbm, unit_ref, conv_q_ref, conv_d_ref, maps_v, sems):
    copies = []
    for block in range(IMAGES // BLOCK):
        here = pl.ds(block * BLOCK, BLOCK)
        copies.append(pltpu.make_async_copy(maps_hbm.at[here], maps_v.at[here], sems.at[block]))
    for copy in copies:
        copy.start()
    near = lax.broadcasted_iota(jnp.int32, (CELLS, CELLS), 0)
    far = lax.broadcasted_iota(jnp.int32, (CELLS, CELLS), 1)
    for tap_ref, out_ref, result, source in (
        (tap_q_ref, conv_q_ref, near, far),
        (tap_d_ref, conv_d_ref, far, near),
    ):
        down = lax.shift_right_logical(source, 4) - lax.shift_right_logical(result, 4)
        right = (source & (GRID - 1)) - (result & (GRID - 1))
        matrix = jnp.zeros((CELLS, CELLS), f32)
        taps = tap_ref[...].astype(f32)
        for i in range(3):
            for j in range(3):
                hit = (down == i - 1) & (right == j - 1)
                matrix = jnp.where(hit, taps[i : i + 1, j : j + 1], matrix)
        out_ref[...] = matrix.astype(bf16)
    for block, copy in enumerate(copies):
        copy.wait()
        for image in range(block * BLOCK, (block + 1) * BLOCK):
            unit_ref[image] = unit(maps_v[image].astype(f32)).astype(bf16)


def prepare_images(database, tap_q, tap_d):
    vmem = pl.BlockSpec(memory_space=pltpu.VMEM)
    square_shape = jax.ShapeDtypeStruct((CELLS, CELLS), bf16)
    return pl.pallas_call(
        images_kernel,
        in_specs=[vmem, vmem, pl.BlockSpec(memory_space=pl.ANY)],
        out_specs=(vmem, vmem, vmem),
        out_shape=(jax.ShapeDtypeStruct(database.shape, bf16), square_shape, square_shape),
        scratch_shapes=[
            pltpu.VMEM(database.shape, bf16),
            pltpu.SemaphoreType.DMA((IMAGES // BLOCK,)),
        ],
        compiler_params=pltpu.CompilerParams(vmem_limit_bytes=12 * 2**20),
        cost_estimate=pl.CostEstimate(flops=2**24, bytes_accessed=20 * 2**20, transcendentals=0),
    )(tap_q, tap_d, database)


def move(array, step):
    return lax.ppermute(array, MAIN, PAIRS[step])


def orders():
    return [(LATE[piece % 3], LATE[(piece + 1) % 3], LATE[(piece + 2) % 3]) for piece in (0, 2, 1)]


def split(held, own):
    pieces = []
    for piece in range(3):
        first = CUTS[piece] + (16 if piece else 0)
        pieces.append(held[:, first : CUTS[piece + 1] + 16])
    came = [move(p, o[0]) for p, o in zip(pieces, orders())]
    pieces = [jnp.concatenate(pair, axis=0) for pair in zip(pieces, came)]
    pieces[0], own = lax.optimization_barrier((pieces[0], own))
    return pieces, own


def sources(combo):
    bits = (combo & 1, combo >> 1 & 1, combo >> 2)
    for turn in (0, 2, 1):
        yield bits[(turn + 1) % 3] + 2 * bits[(turn + 2) % 3], bits[turn]


def pair_kernel(wave, names, place_ref, *refs):
    held = len(WAVES[wave]) * GROUP
    spare = 4 * held
    refs, scratch = refs[:-9], refs[-9:]
    query_v, ids_v, table_v, column_v, peak_v, total_v, table_s, pair_s, sems = scratch
    parts, refs = dict(zip(names, refs)), refs[len(names) :]
    earlier = ()
    if wave == 2:
        earlier, refs = refs[:2], refs[2:]
    if wave == 0:
        own_hbm, other_hbm, conv_q_ref, conv_d_ref, out_ref, image_v = refs[:6]
        image_copies = [
            pltpu.make_async_copy(own_hbm, image_v.at[pl.ds(0, IMAGES)], sems.at[2]),
            pltpu.make_async_copy(other_hbm, image_v.at[pl.ds(IMAGES, IMAGES)], sems.at[3]),
        ]
    else:
        image_v, conv_q_ref, conv_d_ref, out_ref = refs[:4]
        image_copies = []
    id_copies, copies = [], []
    for local, combo in enumerate(WAVES[wave]):
        here = pl.ds(GROUP * local, GROUP)
        for piece, (which, half) in enumerate(sources(combo)):
            source = parts[piece, which]
            blocks = pl.ds(GROUP * half, GROUP)
            size = CUTS[piece + 1] - CUTS[piece]
            skip = 0 if piece else 16
            copies.append(
                pltpu.make_async_copy(
                    source.at[blocks, pl.ds(skip, size), :],
                    query_v.at[here, pl.ds(CUTS[piece], size), :],
                    sems.at[1],
                )
            )
            if piece == 0:
                id_copies.append(
                    pltpu.make_async_copy(
                        source.at[blocks, pl.ds(0, 16), :], ids_v.at[here], sems.at[0]
                    )
                )
    for copy in id_copies + image_copies + copies:
        copy.start()
    pltpu.make_async_copy(ids_v, ids_v, sems.at[0]).wait()
    packed = jnp.sum(ids_v[...].astype(f32), axis=1)
    ids = packed[:, :CAND].astype(jnp.int32) * 64 + packed[:, CAND:].astype(jnp.int32)
    lane = lax.broadcasted_iota(jnp.int32, (held, CAND), 1)
    shard = lax.shift_right_logical(ids, 5)
    slot = ids & (IMAGES - 1)
    table = jnp.full((held, CAND), -1, jnp.int32)
    for side in range(2):
        mine = shard == place_ref[side]
        first = jnp.min(jnp.where(mine, lane, CAND), axis=1, keepdims=True)
        last = jnp.max(jnp.where(mine, lane, -1), axis=1, keepdims=True)
        last = jnp.where(last > first, last, -1)
        for which, column in ((2 * side, first), (2 * side + 1, last)):
            at = lane == column
            image = jnp.max(jnp.where(at, slot, -1), axis=1, keepdims=True)
            image = jnp.where(image >= 0, image + side * IMAGES, -1)
            table = jnp.where(lane == which, image, table)
            column_v[which] = jnp.broadcast_to(column, (held, CAND))
    table_v[...] = table
    move = pltpu.make_async_copy(table_v, table_s, sems.at[4])
    move.start()
    move.wait()

    def fill(query, count):
        for which in range(4):
            image = table_s[query, which]
            pair_s[count] = query * 65536 + (which * held + query) * 64 + jnp.maximum(image, 0)
            count = count + (image >= 0).astype(jnp.int32)
        return count

    count = lax.fori_loop(0, held, fill, jnp.int32(0), unroll=8)
    for extra in range(LARGE):
        pair_s[count + extra] = spare * 64
    for copy in image_copies:
        copy.wait()
    pltpu.make_async_copy(query_v, query_v, sems.at[1]).wait()

    def group(size, base, step, carry):
        found = []
        for part in range(size):
            code = pair_s[base + step * size + part]
            node = lax.shift_right_logical(code, 16)
            image = code & 63
            correlation = jnp.dot(query_v[node], image_v[image], preferred_element_type=f32)
            rectified = jnp.maximum(correlation, 0.0).astype(bf16)
            found.append((lax.shift_right_logical(code, 6) & 1023, rectified))
        for row, rectified in found:
            filtered = jnp.dot(conv_q_ref[...], rectified, preferred_element_type=f32)
            filtered = filtered + jnp.dot(rectified, conv_d_ref[...], preferred_element_type=f32)
            peak_v[pl.ds(row, 1), :] = jnp.max(filtered, axis=0, keepdims=True)
        return carry

    large = (count + LARGE - SMALL - 1) // LARGE
    rest = jnp.maximum(count - large * LARGE, 0)
    lax.fori_loop(0, large, functools.partial(group, LARGE, 0), 0)
    lax.fori_loop(0, (rest + SMALL - 1) // SMALL, functools.partial(group, SMALL, large * LARGE), 0)
    total = jnp.zeros((held, CAND), f32)
    for which in range(4):
        peaks = peak_v[pl.ds(which * held, held), :]
        score = jnp.sum(peaks, axis=1, keepdims=True) * (score_scale / CELLS)
        total = jnp.where(lane == column_v[which], score, total)
    if wave < 2:
        out_ref[...] = total
        return
    done = 0
    for ref in earlier:
        total_v[pl.ds(done, ref.shape[0]), :] = ref[...]
        done += ref.shape[0]
    total_v[pl.ds(done, held), :] = total

    def settle(query, carry):
        out_ref[pl.ds(place_ref[2 + query], 1), :] = total_v[pl.ds(query, 1), :]
        return carry

    lax.fori_loop(0, NODES, settle, 0, unroll=8)


def pair_scores(wave, place, parts, earlier, images, conv_q, conv_d):
    smem = pl.BlockSpec(memory_space=pltpu.SMEM)
    vmem = pl.BlockSpec(memory_space=pltpu.VMEM)
    hbm = pl.BlockSpec(memory_space=pl.ANY)
    held = len(WAVES[wave]) * GROUP
    names = sorted(
        {(piece, which) for combo in WAVES[wave] for piece, (which, _) in enumerate(sources(combo))}
    )
    out_shape = jax.ShapeDtypeStruct((NODES if wave == 2 else held, CAND), f32)
    out_specs = vmem
    image_specs = [vmem]
    if wave == 0:
        out_shape = (out_shape, jax.ShapeDtypeStruct((2 * IMAGES, CELLS, CELLS), bf16))
        out_specs = (vmem, vmem)
        image_specs = [pl.BlockSpec(memory_space=pltpu.HBM)] * 2
    return pl.pallas_call(
        functools.partial(pair_kernel, wave, names),
        out_shape=out_shape,
        in_specs=[smem] + [hbm] * len(names) + [vmem] * len(earlier) + image_specs + [vmem, vmem],
        out_specs=out_specs,
        scratch_shapes=[
            pltpu.VMEM((held, CELLS, CELLS), bf16),
            pltpu.VMEM((held, 16, CELLS), bf16),
            pltpu.VMEM((held, CAND), jnp.int32),
            pltpu.VMEM((4, held, CAND), jnp.int32),
            pltpu.VMEM((4 * held + 8, CELLS), f32),
            pltpu.VMEM((NODES, CAND), f32),
            pltpu.SMEM((held, CAND), jnp.int32),
            pltpu.SMEM((4 * held + LARGE,), jnp.int32),
            pltpu.SemaphoreType.DMA((5,)),
        ],
        compiler_params=pltpu.CompilerParams(vmem_limit_bytes=12 * 2**20),
        cost_estimate=pl.CostEstimate(
            flops=3 * held * 6 * CELLS**3, bytes_accessed=16 * 2**20, transcendentals=0
        ),
    )(place, *[parts[piece][which] for piece, which in names], *earlier, *images, conv_q, conv_d)


def finish_kernel(parts_ref, scores_ref, top_ref):
    row = jnp.sum(parts_ref[...], axis=0, keepdims=True)
    scores_ref[...] = row
    across = jnp.broadcast_to(row, (CAND, CAND))
    down = across.T
    at_row = lax.broadcasted_iota(jnp.int32, (CAND, CAND), 0)
    at_col = lax.broadcasted_iota(jnp.int32, (CAND, CAND), 1)
    ahead = (across > down) | ((across == down) & (at_col < at_row))
    rank = jnp.sum(ahead.astype(f32), axis=1, keepdims=True)
    placed = jnp.where(rank == at_col.astype(f32), down, 0.0)
    top_ref[...] = jnp.sum(placed, axis=0, keepdims=True)[:, :TOPK]


def finish(parts):
    return pl.pallas_call(
        finish_kernel,
        out_shape=(
            jax.ShapeDtypeStruct((1, CAND), f32),
            jax.ShapeDtypeStruct((1, TOPK), f32),
        ),
    )(parts)


def place_table():
    me = lax.axis_index("c")
    x, y, z = [lax.axis_index(axis) for axis in NODE]
    base = (x * 4 + y) * 8 + z
    near = jnp.where(me == 0, 1, 3)
    far = 4 - near
    combos = jnp.array([combo for wave in WAVES for combo in wave], jnp.int32)
    index = (combos[:, None] * GROUP + jnp.arange(GROUP, dtype=jnp.int32)).reshape(-1)
    bit = [lax.shift_right_logical(index, k) & 1 for k in range(6)]
    z = z ^ (bit[0] * near) ^ (bit[4] * far)
    x = x ^ (bit[1] * near) ^ (bit[5] * far)
    y = y ^ (bit[2] * far) ^ (bit[3] * near)
    shards = jnp.stack([base + 4 * me, base + 4 * (1 - me)])
    return jnp.concatenate([shards, (x * 4 + y) * 4 + z]).astype(jnp.int32)


def body(query_maps, database, shortlist, kernel_query, kernel_db):
    held = pack(query_maps, shortlist)
    held = jnp.concatenate([held] + [move(held, step) for step in OPENING], axis=0)
    database, held = lax.optimization_barrier((database, held))
    own, conv_q, conv_d = prepare_images(database, kernel_query, kernel_db)
    place = place_table()
    pieces, own = split(held, own)
    other = lax.ppermute(own, "c", [(0, 1), (1, 0)])
    second = [move(p, o[1]) for p, o in zip(pieces, orders())]
    third = [move(p, o[2]) for p, o in zip(pieces, orders())]
    first_scores, images = pair_scores(
        0, place, [[p] for p in pieces], (), (own, other), conv_q, conv_d
    )
    *second, first_scores = lax.optimization_barrier((*second, first_scores))
    fourth = [move(p, o[2]) for p, o in zip(second, orders())]
    parts = [list(part) for part in zip(pieces, second, third, fourth)]
    second_scores = pair_scores(1, place, parts, (), (images,), conv_q, conv_d)
    earlier = (first_scores, second_scores)
    scores = pair_scores(2, place, parts, earlier, (images,), conv_q, conv_d)
    scores = lax.all_to_all(scores, NODE, split_axis=0, concat_axis=0, tiled=True)
    return finish(scores)


def solution(mesh):
    fine = Mesh(mesh.devices.reshape(4, 4, 2, 4), MAIN)
    in_specs = (P(MAIN, None, None), P(MAIN, None, None), P(MAIN, None), P(), P())
    out_specs = (P(MAIN, None), P(MAIN, None))
    return jax.shard_map(body, mesh=fine, in_specs=in_specs, out_specs=out_specs, check_vma=False)
```
